256 devices in a mesh: rep: 8 (over y, core), fsdp: 32 (over x, z).
Axes of the slice: x: 4, y: 4, z: 8, core: 2. Of those that a mesh axis runs over, the one named last changes fastest.
Arguments:
- grad_parts: bfloat16 [8, 4096, 7168], P('rep', 'fsdp'), may hold values from -1.5 to 1.5
- weights: bfloat16 [4096, 7168], P('fsdp'), may hold values from -1.5 to 1.5
- left_stat: float32 [64, 1024, 1024], P('fsdp', 'rep'), may hold values from -6 to 6
- right_stat: float32 [64, 1024, 1024], P('fsdp', 'rep'), may hold values from -6 to 6
- left_root: bfloat16 [64, 1024, 1024], P('fsdp', 'rep'), may hold values from -0.1875 to 0.1875
- right_root: bfloat16 [64, 1024, 1024], P('fsdp', 'rep'), may hold values from -0.1875 to 0.1875
- adam_moment: float32 [64, 1024, 1024], P('fsdp', 'rep'), may hold values from 0.01 to 0.2
- owner_slot: int32 [28], replicated, may hold values from 0 to 63, as said below
Outputs:
- new_weights: bfloat16 [4096, 7168], P('fsdp')
- new_left: float32 [64, 1024, 1024], P('fsdp', 'rep')
- new_right: float32 [64, 1024, 1024], P('fsdp', 'rep')
- new_moment: float32 [64, 1024, 1024], P('fsdp', 'rep')
The draws below stay inside these ranges and needn't reach their ends.
Inputs may be any that keep to these rules, and one draw needn't show every extreme that they name: `owner_slot`: distinct blocks name distinct slots; the 7 blocks of one row of blocks name distinct owners (owner = slot // 2); an owner holds at most 2 blocks.
All inputs are finite; a program needn't handle non-finite values.
Results may differ from the reference program's by a relative error of at most 0.022.
Values may be sent and summed in bfloat16 or wider, within the bound.
No kernel may reach another device: no remote copies, remote signals or barrier semaphores. Data moves between devices by JAX's collectives and lax.ppermute only.
A program may use at most 128 MiB of HBM per device.

```python
import math
import jax
import jax.numpy as jnp
from jax import lax

D = 7168
BLOCK = 1024
ROWS = 4096
NBLK = 28
CAP = 2
SLOTS = 64
N_REP = 8
N_FSDP = 32


def draw_owner_slot(key, part):
    key = jax.random.fold_in(key, 7)
    order = jax.random.permutation(key, N_FSDP).astype(jnp.int32)
    span = max(D // BLOCK, (NBLK + CAP - 1) // CAP)
    positions = jnp.arange(NBLK, dtype=jnp.int32)
    owners = order[positions % span]
    return (owners * CAP + positions // span).astype(jnp.int32)


def level_of(stream_key, shape, split, low, high):
    gain, own = 1.0, jax.random.fold_in(stream_key, 6)
    for dim, blocks in split:
        heights = jnp.exp(jax.random.uniform(jax.random.fold_in(own, dim), (blocks,), jnp.float32, low / len(split), high / len(split)))
        gain = gain * jnp.repeat(heights, shape[dim] // blocks).reshape([-1 if axis == dim else 1 for axis in range(len(shape))])
    return gain


def gaussian(own_key, extent, deviation, reach, cuts=(), kind=jnp.bfloat16):
    result = jax.random.normal(own_key, extent, jnp.float32) * deviation
    if len(cuts) > 0:
        result = level_of(own_key, extent, cuts, -0.22, 0.18) * result
    return jnp.clip(result, min=-reach, max=reach).astype(kind)


def setup_inputs(seed: int = 0) -> dict:
    keys = jax.random.split(jax.random.key(seed), 9)
    return {
        "grad_parts": gaussian(keys[0], (N_REP, ROWS, D), 0.1, 1.5, ((0, 8), (1, 32))),
        "weights": gaussian(keys[1], (ROWS, D), 0.1, 1.5, ((0, 32),)),
        "left_stat": gaussian(keys[2], (SLOTS, BLOCK, BLOCK), 1.0, 6.0, ((0, 32), (1, 8)), jnp.float32),
        "right_stat": gaussian(keys[3], (SLOTS, BLOCK, BLOCK), 1.0, 6.0, ((0, 32), (1, 8)), jnp.float32),
        "left_root": gaussian(keys[4], (SLOTS, BLOCK, BLOCK), BLOCK ** -0.5, 0.1875, ((0, 32), (1, 8))),
        "right_root": gaussian(keys[5], (SLOTS, BLOCK, BLOCK), BLOCK ** -0.5, 0.1875, ((0, 32), (1, 8))),
        "adam_moment": jnp.clip(jnp.exp(math.log(0.2) - 2.9957323 * jax.random.uniform(keys[6], (SLOTS, BLOCK, BLOCK), jnp.float32) ** level_of(keys[6], (SLOTS, BLOCK, BLOCK), ((0, 32), (1, 8)), -0.2, 0.2)), 0.01, 0.2),
        "owner_slot": draw_owner_slot(jax.random.fold_in(keys[8], 71), 0),
    }


BETA_STAT = 0.95
BETA_ADAM = 0.99
LEARN_RATE = 0.2
ADAM_EPS = 1e-08
NORM_EPS = 1e-06

def slot_table(owner_slot, slot_ids):
    matches = (owner_slot[None, :] == slot_ids[:, None]).astype(jnp.int32)
    positions = jnp.arange(owner_slot.shape[0], dtype=jnp.int32)
    block_ids = lax.optimization_barrier(jnp.sum(matches * positions[None, :], axis=1)).astype(jnp.int32)
    live_mask = lax.optimization_barrier(jnp.sum(matches, axis=1)).astype(jnp.int32)
    return (block_ids, live_mask)

def reference(grad_parts, weights, left_stat, right_stat, left_root, right_root, adam_moment, owner_slot):
    summed = lax.optimization_barrier(jnp.sum(grad_parts.astype(jnp.float32), axis=0)).astype(jnp.bfloat16)
    col_blocks = D // BLOCK
    row_blocks = ROWS // BLOCK
    blocks = summed.reshape(row_blocks, BLOCK, col_blocks, BLOCK).transpose(0, 2, 1, 3).reshape(NBLK, BLOCK, BLOCK)
    block_ids, live_mask = slot_table(owner_slot, jnp.arange(SLOTS, dtype=jnp.int32))

    def per_slot(slot_items):
        left_in, right_in, left_inv, right_inv, moment_in, block_id, live_flag = slot_items
        gradient = lax.dynamic_index_in_dim(blocks, block_id, 0, keepdims=False) * live_flag.astype(jnp.bfloat16)
        gram_left = jnp.dot(gradient, gradient.T, preferred_element_type=jnp.float32)
        gram_right = jnp.dot(gradient.T, gradient, preferred_element_type=jnp.float32)
        left_new = BETA_STAT * left_in + (1.0 - BETA_STAT) * gram_left
        right_new = BETA_STAT * right_in + (1.0 - BETA_STAT) * gram_right
        left_product = jnp.dot(left_inv, gradient, preferred_element_type=jnp.float32).astype(jnp.bfloat16)
        precond = jnp.dot(left_product, right_inv, preferred_element_type=jnp.float32)
        grad_float = gradient.astype(jnp.float32)
        moment = BETA_ADAM * moment_in + (1.0 - BETA_ADAM) * grad_float * grad_float
        adam_step = grad_float / (jnp.sqrt(moment) + ADAM_EPS)
        graft = jnp.sqrt(jnp.sum(adam_step * adam_step) / (jnp.sum(precond * precond) + NORM_EPS))
        slot_step = (-LEARN_RATE * graft * precond).astype(jnp.bfloat16)
        return (left_new, right_new, moment, slot_step)
    new_left, new_right, new_moment, slot_steps = lax.map(per_slot, (left_stat, right_stat, left_root, right_root, adam_moment, block_ids, live_mask))
    block_steps = slot_steps[owner_slot]
    update = block_steps.reshape(row_blocks, col_blocks, BLOCK, BLOCK).transpose(0, 2, 1, 3).reshape(ROWS, D)
    new_weights = (weights.astype(jnp.float32) + update.astype(jnp.float32)).astype(jnp.bfloat16)
    return (new_weights, new_left, new_right, new_moment)
```

```python
import functools

import jax
import jax.numpy as jnp
from jax import lax
from jax.experimental import pallas as pl
from jax.experimental.pallas import tpu as pltpu
from jax.sharding import PartitionSpec as P

BETA_STAT = 0.95
BETA_ADAM = 0.99
LEARN_RATE = 0.2
ADAM_EPS = 1e-08
NORM_EPS = 1e-06
PAD = 128
ANY = pl.BlockSpec(memory_space=pl.ANY)
SMEM = pl.BlockSpec(memory_space=pltpu.SMEM)
VMEM = pl.BlockSpec(memory_space=pltpu.VMEM)
PARAMS = pltpu.CompilerParams(vmem_limit_bytes=40 * 1024 * 1024)


def slot_block(owner_ref, slot):
    def step(b, carry):
        block, live = carry
        hit = owner_ref[b] == slot
        return jnp.where(hit, b, block), jnp.where(hit, 1, live)

    return lax.fori_loop(0, owner_ref.shape[0], step, (jnp.int32(0), jnp.int32(0)))


def pack_kernel(owner_ref, ids_ref, a_ref, b_ref, c_ref, d_ref, out_ref, held, sem):
    capacity, col_blocks, shard_count = ids_ref[2], held.shape[0], ids_ref[3]
    width = held.shape[2]
    row = ids_ref[0] // shard_count
    for j in range(col_blocks):
        cols = slice(j * width, (j + 1) * width)
        total = a_ref[:, cols].astype(jnp.float32) + b_ref[:, cols].astype(jnp.float32)
        total += c_ref[:, cols].astype(jnp.float32) + d_ref[:, cols].astype(jnp.float32)
        held[j] = total.astype(jnp.bfloat16)
        dest = owner_ref[row * col_blocks + j] // capacity
        pltpu.make_async_copy(held.at[j], out_ref.at[dest], sem.at[j]).start()
    for j in range(col_blocks):
        pltpu.make_async_copy(held.at[j], out_ref.at[0], sem.at[j]).wait()


def frame_kernel(owner_ref, ids_ref, in_ref, out_ref, sem):
    shard_count = out_ref.shape[1]
    col_blocks = ids_ref[4]
    for k in range(out_ref.shape[0]):
        block, _ = slot_block(owner_ref, ids_ref[0] * out_ref.shape[0] + k)
        start = (block // col_blocks) * shard_count
        pltpu.make_async_copy(in_ref.at[pl.ds(start, shard_count)], out_ref.at[k], sem.at[k]).start()
    for k in range(out_ref.shape[0]):
        pltpu.make_async_copy(in_ref.at[pl.ds(0, shard_count)], out_ref.at[k], sem.at[k]).wait()


def split3(value):
    high = value.astype(jnp.bfloat16).astype(jnp.float32)
    rest = value - high
    mid = rest.astype(jnp.bfloat16).astype(jnp.float32)
    return high, mid, rest - mid


def step_kernel(
    owner_ref, ids_ref, grad_ref, left_ref, right_ref, moment_ref,
    out_ref, new_moment_ref,
    grad, left, right, moment, fresh, send, in_sem, out_sem,
):
    capacity, shards, reps, piece, width = grad.shape
    size = shards * reps * piece
    band = reps * piece
    rep = ids_ref[1]
    col_blocks = ids_ref[4]
    loads = []
    for k in range(capacity):
        loads.append(
            [pltpu.make_async_copy(left_ref.at[:, k], left.at[k], in_sem.at[k, 0])]
            + [
                pltpu.make_async_copy(grad_ref.at[r, k], grad.at[k, :, r], in_sem.at[k, 4 + r])
                for r in range(reps)
            ]
            + [
                pltpu.make_async_copy(right_ref.at[:, k], right.at[k], in_sem.at[k, 1]),
                pltpu.make_async_copy(moment_ref.at[k], moment.at[k], in_sem.at[k, 2]),
            ]
        )
        for copy in loads[k]:
            copy.start()
    for k in range(capacity):
        block, live = slot_block(owner_ref, ids_ref[0] * capacity + k)
        row = block // col_blocks
        for copy in loads[k]:
            copy.wait()

        @pl.when(live > 0)
        def _():
            whole = grad[k].reshape(size, width)
            product = jnp.dot(
                left[k].reshape(band, size), whole, preferred_element_type=jnp.float32
            ).astype(jnp.bfloat16)
            precond = jnp.dot(
                product, right[k].reshape(size, width), preferred_element_type=jnp.float32
            )
            band_grad = grad[k, rep].reshape(band, width).astype(jnp.float32)
            new = BETA_ADAM * moment[k] + (1.0 - BETA_ADAM) * band_grad * band_grad
            fresh[k] = new
            step = band_grad / (jnp.sqrt(new) + ADAM_EPS)
            parts = split3(jnp.sum(step * step)) + split3(jnp.sum(precond * precond))
            lane = lax.broadcasted_iota(jnp.int32, (shards, piece, PAD), 2)
            extra = jnp.zeros((shards, piece, PAD), jnp.float32)
            for n, part in enumerate(parts):
                extra = jnp.where(lane == n, part, extra)
            send[k, :, :, :width] = precond.astype(jnp.bfloat16).reshape(shards, piece, width)
            send[k, :, :, width:] = extra.astype(jnp.bfloat16)
            pltpu.make_async_copy(
                send.at[k], out_ref.at[pl.ds(row * shards, shards)], out_sem.at[k, 0]
            ).start()

        @pl.when(live == 0)
        def _():
            fresh[k] = BETA_ADAM * moment[k]

        pltpu.make_async_copy(fresh.at[k], new_moment_ref.at[k], out_sem.at[k, 1]).start()
    for k in range(capacity):
        _, live = slot_block(owner_ref, ids_ref[0] * capacity + k)

        @pl.when(live > 0)
        def _():
            pltpu.make_async_copy(
                send.at[k], out_ref.at[pl.ds(0, shards)], out_sem.at[k, 0]
            ).wait()

        pltpu.make_async_copy(fresh.at[k], new_moment_ref.at[k], out_sem.at[k, 1]).wait()


def stat_kernel(
    owner_ref, ids_ref, grad_ref, left_ref, right_ref, new_left_ref, new_right_ref, grad, sem
):
    k = pl.program_id(0)
    shards, reps, piece, width = grad.shape
    size = shards * reps * piece
    band = reps * piece
    rep = ids_ref[1]
    copies = [
        pltpu.make_async_copy(grad_ref.at[r, k], grad.at[:, r], sem.at[r]) for r in range(reps)
    ]
    for copy in copies:
        copy.start()
    _, live = slot_block(owner_ref, ids_ref[0] * pl.num_programs(0) + k)
    for copy in copies:
        copy.wait()

    @pl.when(live > 0)
    def _():
        whole = grad[...].reshape(size, width)
        rows = grad[rep].reshape(band, width)
        gram = lax.dot_general(
            rows, whole, (((1,), (1,)), ((), ())), preferred_element_type=jnp.float32
        )
        new_left_ref[0] = BETA_STAT * left_ref[0] + (1.0 - BETA_STAT) * gram
        cols = grad[:, :, :, pl.ds(pl.multiple_of(rep * band, band), band)].reshape(size, band)
        gram = lax.dot_general(
            cols, whole, (((0,), (0,)), ((), ())), preferred_element_type=jnp.float32
        )
        new_right_ref[0] = BETA_STAT * right_ref[0] + (1.0 - BETA_STAT) * gram

    @pl.when(live == 0)
    def _():
        new_left_ref[0] = BETA_STAT * left_ref[0]
        new_right_ref[0] = BETA_STAT * right_ref[0]


def collect_kernel(owner_ref, ids_ref, in_ref, out_ref, sem):
    capacity, shard_count, col_blocks = ids_ref[2], ids_ref[3], sem.shape[0]
    width = in_ref.shape[2]
    row = ids_ref[0] // shard_count
    for j in range(col_blocks):
        source = owner_ref[row * col_blocks + j] // capacity
        pltpu.make_async_copy(
            in_ref.at[source], out_ref.at[:, pl.ds(j * width, width)], sem.at[j]
        ).start()
    for j in range(col_blocks):
        pltpu.make_async_copy(
            in_ref.at[0], out_ref.at[:, pl.ds(j * width, width)], sem.at[j]
        ).wait()


def finish_kernel(weights_ref, *refs):
    out_ref = refs[-1]
    parts, order_ref = refs[:-2], refs[-2]
    piece = parts[0].shape[0]
    width = out_ref.shape[1]
    extra = jnp.zeros((1, PAD), jnp.float32)
    for part in parts:
        extra += part[:1, width:].astype(jnp.float32)
    lane = lax.broadcasted_iota(jnp.int32, extra.shape, 1)
    adam = jnp.sum(jnp.where(lane < 3, extra, 0.0))
    norm = jnp.sum(jnp.where((lane >= 3) & (lane < 6), extra, 0.0))
    scale = -LEARN_RATE * jnp.sqrt(jnp.full((1, 1), adam) / (jnp.full((1, 1), norm) + NORM_EPS))
    for n, part in enumerate(parts):
        rows = pl.ds(pl.multiple_of(order_ref[n] * piece, piece), piece)
        out_ref[rows, :] = (
            weights_ref[rows, :].astype(jnp.float32) + scale * part[:, :width].astype(jnp.float32)
        ).astype(jnp.bfloat16)


def local(
    grad_parts, weights, left_stat, right_stat, left_root, right_root, adam_moment, owner_slot
):
    rep = lax.axis_index("rep")
    own = lax.axis_index("fsdp")
    n_rep, n_fsdp = lax.axis_size("rep"), lax.axis_size("fsdp")
    capacity, band, size = left_stat.shape
    rows, full = grad_parts.shape[1:]
    col_blocks = full // size
    shards = size // rows
    piece = rows // n_rep
    n_y = n_rep // 2
    y, core = rep // 2, rep % 2
    ids = jnp.stack([own, rep, jnp.int32(capacity), jnp.int32(shards), jnp.int32(col_blocks)])
    ids = ids.astype(jnp.int32)
    bf16 = jnp.bfloat16

    def along_y(value, shift):
        return lax.ppermute(
            value, "rep", [(i, (i + 2 * shift) % n_rep) for i in range(n_rep)]
        )

    def across(value):
        return lax.ppermute(value, "rep", [(i, i ^ 1) for i in range(n_rep)])

    shard = grad_parts[0].reshape(n_y, 2, piece, full)
    mine = lax.dynamic_index_in_dim(shard, core, 1, keepdims=False)
    other = lax.dynamic_index_in_dim(shard, 1 - core, 1, keepdims=False)
    pair = (mine.astype(jnp.float32) + across(other).astype(jnp.float32)).astype(bf16)
    terms = [lax.dynamic_index_in_dim(pair, y, 0, keepdims=False)]
    for shift in range(1, n_y):
        part = lax.dynamic_index_in_dim(pair, (y + shift) % n_y, 0, keepdims=False)
        terms.append(along_y(part, shift))

    pieces = pl.pallas_call(
        pack_kernel,
        out_shape=jax.ShapeDtypeStruct((n_fsdp, piece, size), bf16),
        in_specs=[SMEM, SMEM] + [VMEM] * 4,
        out_specs=ANY,
        scratch_shapes=[
            pltpu.VMEM((col_blocks, piece, size), bf16),
            pltpu.SemaphoreType.DMA((col_blocks,)),
        ],
        compiler_params=PARAMS,
        name="pack",
    )(owner_slot, ids, *terms)
    arrived = lax.all_to_all(pieces, "fsdp", 0, 0, tiled=True)
    frames = pl.pallas_call(
        frame_kernel,
        out_shape=jax.ShapeDtypeStruct((capacity, shards, piece, size), bf16),
        in_specs=[SMEM, SMEM, ANY],
        out_specs=ANY,
        scratch_shapes=[pltpu.SemaphoreType.DMA((capacity,))],
        compiler_params=PARAMS,
        name="frames",
    )(owner_slot, ids, arrived)
    gradient = lax.all_gather(frames, "rep", axis=0)

    left_rows = lax.all_to_all(
        left_root.reshape(capacity, n_rep, piece, size).transpose(1, 0, 2, 3),
        "rep", 0, 0, tiled=True,
    )
    right_full = lax.all_gather(right_root, "rep", axis=0)

    sendback, new_moment = pl.pallas_call(
        step_kernel,
        out_shape=(
            jax.ShapeDtypeStruct((n_fsdp, piece, size + PAD), bf16),
            jax.ShapeDtypeStruct(adam_moment.shape, jnp.float32),
        ),
        in_specs=[SMEM, SMEM] + [ANY] * 4,
        out_specs=(ANY, ANY),
        scratch_shapes=[
            pltpu.VMEM((capacity, shards, n_rep, piece, size), bf16),
            pltpu.VMEM((capacity, n_rep, piece, size), bf16),
            pltpu.VMEM((capacity, n_rep, band, size), bf16),
            pltpu.VMEM((capacity, band, size), jnp.float32),
            pltpu.VMEM((capacity, band, size), jnp.float32),
            pltpu.VMEM((capacity, shards, piece, size + PAD), bf16),
            pltpu.SemaphoreType.DMA((capacity, 4 + n_rep)),
            pltpu.SemaphoreType.DMA((capacity, 2)),
        ],
        compiler_params=PARAMS,
        name="step",
    )(owner_slot, ids, gradient, left_rows, right_full, adam_moment)
    returned = lax.all_to_all(sendback, "fsdp", 0, 0, tiled=True)

    stat = pl.BlockSpec((1, band, size), lambda k: (k, 0, 0))
    new_left, new_right = pl.pallas_call(
        stat_kernel,
        grid=(capacity,),
        out_shape=(
            jax.ShapeDtypeStruct(left_stat.shape, jnp.float32),
            jax.ShapeDtypeStruct(right_stat.shape, jnp.float32),
        ),
        in_specs=[SMEM, SMEM, ANY, stat, stat],
        out_specs=(stat, stat),
        scratch_shapes=[
            pltpu.VMEM((shards, n_rep, piece, size), bf16),
            pltpu.SemaphoreType.DMA((n_rep,)),
        ],
        compiler_params=PARAMS,
        cost_estimate=pl.CostEstimate(
            flops=8 * capacity * band * size * size,
            bytes_accessed=capacity * size * (16 * band + 2 * size),
            transcendentals=0,
        ),
        name="statistics",
    )(owner_slot, ids, gradient, left_stat, right_stat)

    update = pl.pallas_call(
        collect_kernel,
        out_shape=jax.ShapeDtypeStruct((piece, col_blocks * (size + PAD)), bf16),
        in_specs=[SMEM, SMEM, ANY],
        out_specs=ANY,
        scratch_shapes=[pltpu.SemaphoreType.DMA((col_blocks,))],
        compiler_params=PARAMS,
        name="collect",
    )(owner_slot, ids, returned)
    held = [update] + [along_y(update, shift) for shift in range(1, n_y)]
    held += [across(value) for value in held]
    sources = [((y - shift) % n_y) * 2 + core for shift in range(n_y)]
    sources += [((y - shift) % n_y) * 2 + 1 - core for shift in range(n_y)]
    part = pl.BlockSpec((piece, size + PAD), lambda j: (0, j))
    plane = pl.BlockSpec((rows, size), lambda j: (0, j))
    new_weights = pl.pallas_call(
        finish_kernel,
        grid=(col_blocks,),
        out_shape=jax.ShapeDtypeStruct(weights.shape, bf16),
        in_specs=[plane] + [part] * n_rep + [SMEM],
        out_specs=plane,
        compiler_params=PARAMS,
        name="finish",
    )(weights, *held, jnp.stack(sources).astype(jnp.int32))
    return (new_weights, new_left, new_right, new_moment)


def solution(mesh):
    return jax.shard_map(
        local,
        mesh=mesh,
        in_specs=(
            P("rep", "fsdp", None),
            P("fsdp", None),
            P("fsdp", "rep", None),
            P("fsdp", "rep", None),
            P("fsdp", "rep", None),
            P("fsdp", "rep", None),
            P("fsdp", "rep", None),
            P(),
        ),
        out_specs=(
            P("fsdp", None),
            P("fsdp", "rep", None),
            P("fsdp", "rep", None),
            P("fsdp", "rep", None),
        ),
        check_vma=False,
    )
```

```python
import jax
import jax.numpy as jnp
from jax import lax
from jax.experimental import pallas as pl
from jax.experimental.pallas import tpu as pltpu
from jax.sharding import PartitionSpec as P

BETA_STAT = 0.95
BETA_ADAM = 0.99
LEARN_RATE = 0.2
ADAM_EPS = 1e-08
NORM_EPS = 1e-06
PAD = 128
N_X = 4
REP_ORDER = (0, 4, 2, 6, 1, 5, 3, 7)
ANY = pl.BlockSpec(memory_space=pl.ANY)
HBM = pl.BlockSpec(memory_space=pltpu.HBM)
SMEM = pl.BlockSpec(memory_space=pltpu.SMEM)
VMEM = pl.BlockSpec(memory_space=pltpu.VMEM)
SMALL = pltpu.CompilerParams(vmem_limit_bytes=16 * 1024 * 1024)
LARGE = pltpu.CompilerParams(vmem_limit_bytes=60 * 1024 * 1024)
BF16 = jnp.bfloat16
F32 = jnp.float32


def struct(shape, dtype=BF16):
    return jax.ShapeDtypeStruct(shape, dtype)


def along_z_place(z, n_z, core):
    return jnp.where(core == 0, z, n_z - 1 - z)


def column(index, width):
    return pl.ds(pl.multiple_of(index * width, width), width)


def split_kernel(place_ref, grad_ref, mine_ref, other_ref, sem):
    n_y, col_blocks, _, width = other_ref.shape
    y, core = place_ref[0], place_ref[1]
    copies = []
    for n, out_ref in enumerate((other_ref, mine_ref)):
        for d in range(n_y):
            for j in range(col_blocks):
                index = j * 2 * n_y + lax.rem(y + d, n_y) * 2 + (core if n else 1 - core)
                copies.append(
                    pltpu.make_async_copy(
                        grad_ref.at[:, column(index, width)], out_ref.at[d, j], sem.at[n, d, j]
                    )
                )
                copies[-1].start()
    for copy in copies:
        copy.wait()


def pair_kernel(mine_ref, got_ref, *out_refs):
    for d, out_ref in enumerate(out_refs):
        out_ref[...] = (mine_ref[d].astype(F32) + got_ref[d].astype(F32)).astype(BF16)


def sum_kernel(*refs):
    terms, out_ref = refs[:-2], refs[-1]
    total = terms[0][...].astype(F32)
    for term in terms[1:]:
        total += term[...].astype(F32)
    out_ref[...] = total.astype(BF16)


def turn_kernel(moment_ref, after_ref, out_ref):
    n_rep, capacity, _, width = out_ref.shape
    for r in range(n_rep):
        for k in range(capacity):
            cols = slice(r * width, (r + 1) * width)
            out_ref[REP_ORDER.index(r), k] = moment_ref[k, :, cols].astype(BF16)


def select_kernel(place_ref, table_ref, *refs):
    pieces, out_ref = refs[:-2], refs[-1]
    n_z, capacity = out_ref.shape[:2]
    n_x, col_blocks = len(pieces), pieces[0].shape[0]
    x = place_ref[2]
    for z in range(n_z):
        for k in range(capacity):
            at = along_z_place(z, n_z, place_ref[1])
            block = jnp.maximum(table_ref[(x * n_z + at) * capacity + k], 0)
            row = block // col_blocks
            col = block - row * col_blocks
            shift = lax.rem(x - row + n_x, n_x)
            value = pieces[0][col]
            for d in range(1, n_x):
                value = jnp.where(shift == d, pieces[d][col], value)
            out_ref[z, k] = value


def left_kernel(place_ref, grad_ref, left_ref, out_ref, grad, left, out, in_sem, out_sem):
    n_rep, capacity, band, width = out.shape
    shards, _, rows = grad.shape[:3]
    size = shards * rows
    piece = rows // n_rep
    half = n_rep // 2
    gets = []
    for k in range(capacity):
        if k == 0:
            for s in range(shards):
                at = along_z_place(s, shards, place_ref[1])
                gets.append(pltpu.make_async_copy(grad_ref.at[at], grad.at[s], in_sem.at[0, s]))
        for h in range(2):
            part = pl.ds(h * half, half)
            gets.append(
                pltpu.make_async_copy(left_ref.at[part, k], left.at[k, part], in_sem.at[1 + k, h])
            )
    for copy in gets:
        copy.start()
    for copy in gets[:shards]:
        copy.wait()
    for k in range(capacity):
        whole = grad[:, k].reshape(size, width)
        for h in range(2):
            gets[shards + 2 * k + h].wait()
            part = slice(h * half, (h + 1) * half)
            product = jnp.dot(
                left[k, part].reshape(half * band, size), whole, preferred_element_type=F32
            ).astype(BF16)
            product = product.reshape(half * band // rows, n_rep, piece, width)
            for r in range(n_rep):
                rows_r = slice(h * band // 2, (h + 1) * band // 2)
                out[REP_ORDER.index(r), k, rows_r] = product[:, r].reshape(band // 2, width)
        pltpu.make_async_copy(out.at[:, k], out_ref.at[:, k], out_sem.at[k]).start()
    for k in range(capacity):
        pltpu.make_async_copy(out.at[:, k], out_ref.at[:, k], out_sem.at[k]).wait()


def split3(value):
    high = value.astype(BF16).astype(F32)
    rest = value - high
    mid = rest.astype(BF16).astype(F32)
    return high, mid, rest - mid


def step_kernel(
    place_ref, table_ref, product_ref, right_ref, grad_ref, moment_ref, out_ref,
    product, right, grad, moment, out, in_sem, out_sem,
):
    n_rep, capacity, band, width = product.shape
    size = n_rep * width
    shards, _, piece = out.shape[:3]
    gets = []
    for s in range(shards):
        at = along_z_place(s, shards, place_ref[1])
        gets.append(pltpu.make_async_copy(grad_ref.at[at], grad.at[s], in_sem.at[0, s]))
    for p, r in enumerate(REP_ORDER):
        gets.append(pltpu.make_async_copy(moment_ref.at[p], moment.at[r], in_sem.at[1, r]))
    first = len(gets)
    half = n_rep // 2
    for k in range(capacity):
        if k == 0:
            gets.append(pltpu.make_async_copy(product_ref, product, in_sem.at[2, n_rep - 1]))
        for h in range(2):
            part = pl.ds(h * half, half)
            gets.append(
                pltpu.make_async_copy(
                    right_ref.at[part, k], right.at[k, part], in_sem.at[2 + k, h]
                )
            )
    for copy in gets:
        copy.start()
    for copy in gets[:first]:
        copy.wait()
    norms = []
    for k in range(capacity):
        live = table_ref[place_ref[3] * capacity + k] >= 0
        grad_k = grad[:, k].reshape(size, width).astype(F32)
        grad_k = jnp.where(live, grad_k, 0.0)
        moment_k = moment[:, k].reshape(size, width).astype(F32)
        moment_k = BETA_ADAM * moment_k + (1.0 - BETA_ADAM) * grad_k * grad_k
        step = grad_k / (jnp.sqrt(moment_k) + ADAM_EPS)
        norms.append(jnp.sum(step * step))
    gets[first].wait()
    for k in range(capacity):
        rows = jnp.concatenate(
            [product[REP_ORDER.index(r), k] for r in range(n_rep)], axis=1
        )
        for h in range(2):
            gets[first + 1 + 2 * k + h].wait()
        precond = jnp.dot(rows, right[k].reshape(size, size), preferred_element_type=F32)
        parts = split3(norms[k]) + split3(jnp.sum(precond * precond))
        lane = lax.broadcasted_iota(jnp.int32, (piece, PAD), 1)
        extra = jnp.zeros((piece, PAD), F32)
        for n, part in enumerate(parts):
            extra = jnp.where(lane == n, part, extra)
        extra = extra.astype(BF16)
        precond = precond.astype(BF16).reshape(shards, piece, size)
        for s in range(shards):
            at = along_z_place(s, shards, place_ref[1])
            out[at, k, :, :size] = precond[s]
            out[at, k, :, size:] = extra
        pltpu.make_async_copy(out.at[:, k], out_ref.at[:, k], out_sem.at[k]).start()
    for k in range(capacity):
        pltpu.make_async_copy(out.at[:, k], out_ref.at[:, k], out_sem.at[k]).wait()


def deal_kernel(place_ref, owner_ref, in_ref, *out_refs):
    n_z, capacity = in_ref.shape[:2]
    n_x, col_blocks = len(out_refs), out_refs[0].shape[0]
    for d in range(n_x):
        row = lax.rem(place_ref[2] + d, n_x)
        for j in range(col_blocks):
            slot = owner_ref[row * col_blocks + j]
            owner = slot // capacity
            at = along_z_place(lax.rem(owner, n_z), n_z, place_ref[1])
            out_refs[d][j] = in_ref[at, lax.rem(slot, capacity)]


def collect_kernel(place_ref, owner_ref, *refs):
    pieces, out_ref = refs[:-2], refs[-1]
    n_x, col_blocks, _, width = len(pieces), *pieces[0].shape
    x = place_ref[2]
    for j in range(col_blocks):
        line = owner_ref[x * col_blocks + j] // place_ref[4]
        shift = lax.rem(x - line + n_x, n_x)
        value = pieces[0][j]
        for d in range(1, n_x):
            value = jnp.where(shift == d, pieces[d][j], value)
        out_ref[:, j * width : (j + 1) * width] = value


def stat_kernel(
    place_ref, table_ref, grad_ref, left_ref, right_ref, moment_ref,
    new_left_ref, new_right_ref, new_moment_ref, grad, sem,
):
    k = pl.program_id(0)
    n_rep, shards, _, rows, width = grad_ref.shape
    size = shards * rows
    rep = place_ref[0] * 2 + place_ref[1]
    copies = [
        pltpu.make_async_copy(
            grad_ref.at[r, s if r % 2 == 0 else shards - 1 - s, k],
            grad.at[s, :, pl.ds(r * width, width)],
            sem.at[r, s],
        )
        for r in range(n_rep)
        for s in range(shards)
    ]
    for copy in copies:
        copy.start()
    live = table_ref[place_ref[3] * pl.num_programs(0) + k] >= 0
    for copy in copies:
        copy.wait()

    @pl.when(live)
    def _():
        whole = grad[...].reshape(size, size)
        band = grad[rep]
        gram = lax.dot_general(band, whole, (((1,), (1,)), ((), ())), preferred_element_type=F32)
        new_left_ref[0] = BETA_STAT * left_ref[0] + (1.0 - BETA_STAT) * gram
        cols = grad[:, :, column(rep, width)].reshape(size, width)
        gram = lax.dot_general(cols, whole, (((0,), (0,)), ((), ())), preferred_element_type=F32)
        new_right_ref[0] = BETA_STAT * right_ref[0] + (1.0 - BETA_STAT) * gram
        band = band.astype(F32)
        new_moment_ref[0] = BETA_ADAM * moment_ref[0] + (1.0 - BETA_ADAM) * band * band

    @pl.when(jnp.logical_not(live))
    def _():
        new_left_ref[0] = BETA_STAT * left_ref[0]
        new_right_ref[0] = BETA_STAT * right_ref[0]
        new_moment_ref[0] = BETA_ADAM * moment_ref[0]


def finish_kernel(order_ref, weights_ref, *refs):
    parts, out_ref, out, sem = refs[:-3], refs[-3], refs[-2], refs[-1]
    piece = parts[0].shape[0]
    col_blocks, width = sem.shape[0], parts[0].shape[1] // sem.shape[0]
    size = width - PAD
    lane = lax.broadcasted_iota(jnp.int32, (1, PAD), 1)
    copies = []
    for j in range(col_blocks):
        start = j * width
        extra = jnp.zeros((1, PAD), F32)
        for part in parts:
            extra += part[:1, start + size : start + width].astype(F32)
        adam = jnp.sum(jnp.where(lane < 3, extra, 0.0), axis=1, keepdims=True)
        norm = jnp.sum(jnp.where((lane >= 3) & (lane < 6), extra, 0.0), axis=1, keepdims=True)
        scale = -LEARN_RATE * jnp.sqrt(adam / (norm + NORM_EPS))
        cols = slice(j * size, (j + 1) * size)
        for n, part in enumerate(parts):
            rows = column(order_ref[n], piece)
            out[rows, cols] = (
                weights_ref[rows, cols].astype(F32)
                + scale * part[:, start : start + size].astype(F32)
            ).astype(BF16)
        copies.append(pltpu.make_async_copy(out.at[:, cols], out_ref.at[:, cols], sem.at[j]))
        copies[-1].start()
    for copy in copies:
        copy.wait()


def local(
    grad_parts, weights, left_stat, right_stat, left_root, right_root, adam_moment, owner_slot
):
    rep = lax.axis_index("rep")
    own = lax.axis_index("fsdp")
    n_rep, n_fsdp = lax.axis_size("rep"), lax.axis_size("fsdp")
    n_y, n_x = n_rep // 2, N_X
    n_z = n_fsdp // n_x
    capacity, band, size = left_stat.shape
    rows, full = grad_parts.shape[1:]
    col_blocks = full // size
    width = size // n_rep
    piece = rows // n_rep
    y, core, x = rep // 2, rep % 2, own // n_z
    place = jnp.stack([y, core, x, own, jnp.int32(n_z * capacity)]).astype(jnp.int32)
    slots = jnp.arange(n_fsdp * capacity, dtype=jnp.int32)
    blocks = jnp.arange(owner_slot.shape[0], dtype=jnp.int32)
    table = jnp.max(jnp.where(slots[:, None] == owner_slot[None, :], blocks[None, :], -1), axis=1)
    members = {0: range(n_z), 1: range(n_z - 1, -1, -1)}
    z_lines = [
        [(r * n_x + a) * n_z + b for b in members[r % 2]] for r in range(n_rep) for a in range(n_x)
    ]
    rep_lines = [[r * n_fsdp + a for r in REP_ORDER] for a in range(n_fsdp)]
    axes = ("rep", "fsdp")

    def along_y(value, shift):
        return lax.ppermute(value, "rep", [(i, (i + 2 * shift) % n_rep) for i in range(n_rep)])

    def across(value):
        return lax.ppermute(value, "rep", [(i, i ^ 1) for i in range(n_rep)])

    def along_x(value, shift):
        return lax.ppermute(
            value, "fsdp", [(i, (i + n_z * shift) % n_fsdp) for i in range(n_fsdp)]
        )

    def along_z(value):
        return lax.all_to_all(value, axes, 0, 0, tiled=True, axis_index_groups=z_lines)

    def over_rep(value):
        return lax.all_to_all(value, axes, 0, 0, tiled=True, axis_index_groups=rep_lines)

    left_full = lax.all_gather(left_root, "rep", axis=0)
    right_full = lax.all_gather(right_root, "rep", axis=0)

    shard = grad_parts[0]
    mine, other = pl.pallas_call(
        split_kernel,
        out_shape=[struct((n_y, col_blocks, rows, width))] * 2,
        in_specs=[SMEM, HBM],
        out_specs=[VMEM] * 2,
        scratch_shapes=[pltpu.SemaphoreType.DMA((2, n_y, col_blocks))],
        compiler_params=SMALL,
        name="split",
    )(place, shard)
    pairs = pl.pallas_call(
        pair_kernel,
        out_shape=[struct((col_blocks, rows, width))] * n_y,
        in_specs=[VMEM, VMEM],
        out_specs=[VMEM] * n_y,
        compiler_params=SMALL,
        name="pair",
    )(mine, across(other))
    terms = [pairs[0]] + [along_y(pairs[d], d) for d in range(1, n_y)]
    moment_cols = pl.pallas_call(
        turn_kernel,
        out_shape=struct((n_rep, capacity, band, width)),
        in_specs=[VMEM, ANY],
        out_specs=VMEM,
        compiler_params=SMALL,
        name="turn",
    )(adam_moment, pairs[0])
    summed = pl.pallas_call(
        sum_kernel,
        out_shape=struct((col_blocks, rows, width)),
        in_specs=[VMEM] * n_y + [ANY],
        out_specs=VMEM,
        compiler_params=SMALL,
        name="sum",
    )(*terms, moment_cols)
    moment_cols = over_rep(moment_cols)

    lines = [summed] + [along_x(summed, d) for d in range(1, n_x)]
    routed = along_z(
        pl.pallas_call(
            select_kernel,
            out_shape=struct((n_z, capacity, rows, width)),
            in_specs=[SMEM, SMEM] + [VMEM] * n_x + [ANY],
            out_specs=VMEM,
            compiler_params=SMALL,
            name="select",
        )(place, table, *lines, moment_cols)
    )

    product = pl.pallas_call(
        left_kernel,
        out_shape=struct((n_rep, capacity, band, width)),
        in_specs=[SMEM, HBM, HBM],
        out_specs=HBM,
        scratch_shapes=[
            pltpu.VMEM((n_z, capacity, rows, width), BF16),
            pltpu.VMEM((capacity, n_rep, band, size), BF16),
            pltpu.VMEM((n_rep, capacity, band, width), BF16),
            pltpu.SemaphoreType.DMA((1 + capacity, n_z)),
            pltpu.SemaphoreType.DMA((capacity,)),
        ],
        compiler_params=LARGE,
        name="left",
    )(place, routed, left_full)
    product = over_rep(product)
    steps = pl.pallas_call(
        step_kernel,
        out_shape=struct((n_z, capacity, piece, size + PAD)),
        in_specs=[SMEM, SMEM] + [HBM] * 4,
        out_specs=HBM,
        scratch_shapes=[
            pltpu.VMEM((n_rep, capacity, band, width), BF16),
            pltpu.VMEM((capacity, n_rep, band, size), BF16),
            pltpu.VMEM((n_z, capacity, rows, width), BF16),
            pltpu.VMEM((n_rep, capacity, band, width), BF16),
            pltpu.VMEM((n_z, capacity, piece, size + PAD), BF16),
            pltpu.SemaphoreType.DMA((2 + capacity, n_rep)),
            pltpu.SemaphoreType.DMA((capacity,)),
        ],
        compiler_params=LARGE,
        name="step",
    )(place, table, product, right_full, routed, moment_cols)

    gradient = lax.all_gather(routed, "rep", axis=0)
    stat = pl.BlockSpec((1, band, size), lambda k: (k, 0, 0))
    new_left, new_right, new_moment = pl.pallas_call(
        stat_kernel,
        grid=(capacity,),
        out_shape=[struct(left_stat.shape, F32)] * 3,
        in_specs=[SMEM, SMEM, HBM, stat, stat, stat],
        out_specs=[stat] * 3,
        scratch_shapes=[
            pltpu.VMEM((n_z, rows, size), BF16),
            pltpu.SemaphoreType.DMA((n_rep, n_z)),
        ],
        compiler_params=LARGE,
        cost_estimate=pl.CostEstimate(
            flops=8 * capacity * band * size * size,
            bytes_accessed=capacity * size * (24 * band + 2 * size),
            transcendentals=0,
        ),
        name="statistics",
    )(place, table, gradient, left_stat, right_stat, adam_moment)
    returned = along_z(steps)
    dealt = pl.pallas_call(
        deal_kernel,
        out_shape=[struct((col_blocks, piece, size + PAD))] * n_x,
        in_specs=[SMEM, SMEM, VMEM],
        out_specs=[VMEM] * n_x,
        compiler_params=SMALL,
        name="deal",
    )(place, owner_slot, returned)
    dealt = [dealt[0]] + [along_x(dealt[d], d) for d in range(1, n_x)]
    update = pl.pallas_call(
        collect_kernel,
        out_shape=struct((piece, col_blocks * (size + PAD))),
        in_specs=[SMEM, SMEM] + [VMEM] * n_x + [ANY],
        out_specs=VMEM,
        compiler_params=SMALL,
        name="collect",
    )(place, owner_slot, *dealt, new_moment)
    held = [update] + [along_y(update, d) for d in range(1, n_y)]
    held += [across(value) for value in held]
    sources = [((y - d) % n_y) * 2 + core for d in range(n_y)]
    sources += [((y - d) % n_y) * 2 + 1 - core for d in range(n_y)]
    new_weights = pl.pallas_call(
        finish_kernel,
        out_shape=struct(weights.shape),
        in_specs=[SMEM] + [VMEM] * (1 + n_rep),
        out_specs=HBM,
        scratch_shapes=[pltpu.VMEM(weights.shape, BF16), pltpu.SemaphoreType.DMA((col_blocks,))],
        compiler_params=SMALL,
        name="finish",
    )(jnp.stack(sources).astype(jnp.int32), weights, *held)
    return (new_weights, new_left, new_right, new_moment)


def solution(mesh):
    return jax.shard_map(
        local,
        mesh=mesh,
        in_specs=(
            P("rep", "fsdp", None),
            P("fsdp", None),
            P("fsdp", "rep", None),
            P("fsdp", "rep", None),
            P("fsdp", "rep", None),
            P("fsdp", "rep", None),
            P("fsdp", "rep", None),
            P(),
        ),
        out_specs=(
            P("fsdp", None),
            P("fsdp", "rep", None),
            P("fsdp", "rep", None),
            P("fsdp", "rep", None),
        ),
        check_vma=False,
    )
```

```python
import jax
import jax.numpy as jnp
from jax import lax
from jax.experimental import pallas as pl
from jax.experimental.pallas import tpu as pltpu
from jax.sharding import PartitionSpec as P

BETA_STAT = 0.95
BETA_ADAM = 0.99
LEARN_RATE = 0.2
ADAM_EPS = 1e-08
NORM_EPS = 1e-06
PAD = 128
N_X = 4
REP_ORDER = (0, 4, 2, 6, 1, 5, 3, 7)
ANY = pl.BlockSpec(memory_space=pl.ANY)
HBM = pl.BlockSpec(memory_space=pltpu.HBM)
SMEM = pl.BlockSpec(memory_space=pltpu.SMEM)
VMEM = pl.BlockSpec(memory_space=pltpu.VMEM)
SMALL = pltpu.CompilerParams(vmem_limit_bytes=16 * 1024 * 1024)
LARGE = pltpu.CompilerParams(vmem_limit_bytes=60 * 1024 * 1024)
BF16 = jnp.bfloat16
F32 = jnp.float32


def struct(shape, dtype=BF16):
    return jax.ShapeDtypeStruct(shape, dtype)


def along_z_place(z, n_z, core):
    return jnp.where(core == 0, z, n_z - 1 - z)


def column(index, width):
    return pl.ds(pl.multiple_of(index * width, width), width)


def split_kernel(place_ref, grad_ref, mine_ref, other_ref, sem):
    n_y, col_blocks, _, width = other_ref.shape
    y, core = place_ref[0], place_ref[1]
    copies = []
    for n, out_ref in enumerate((other_ref, mine_ref)):
        for d in range(n_y):
            for j in range(col_blocks):
                index = j * 2 * n_y + lax.rem(y + d, n_y) * 2 + (core if n else 1 - core)
                copies.append(
                    pltpu.make_async_copy(
                        grad_ref.at[:, column(index, width)], out_ref.at[d, j], sem.at[n, d, j]
                    )
                )
                copies[-1].start()
    for copy in copies:
        copy.wait()


def pair_kernel(mine_ref, got_ref, *out_refs):
    for d, out_ref in enumerate(out_refs):
        out_ref[...] = (mine_ref[d].astype(F32) + got_ref[d].astype(F32)).astype(BF16)


def sum_kernel(*refs):
    terms, out_ref = refs[:-2], refs[-1]
    total = terms[0][...].astype(F32)
    for term in terms[1:]:
        total += term[...].astype(F32)
    out_ref[...] = total.astype(BF16)


def turn_kernel(moment_ref, after_ref, out_ref):
    n_rep, capacity, _, width = out_ref.shape
    for r in range(n_rep):
        for k in range(capacity):
            cols = slice(r * width, (r + 1) * width)
            out_ref[REP_ORDER.index(r), k] = moment_ref[k, :, cols].astype(BF16)


def select_kernel(place_ref, table_ref, *refs):
    pieces, out_ref = refs[:-2], refs[-1]
    n_z, capacity = out_ref.shape[:2]
    n_x, col_blocks = len(pieces), pieces[0].shape[0]
    x = place_ref[2]
    for z in range(n_z):
        for k in range(capacity):
            at = along_z_place(z, n_z, place_ref[1])
            block = jnp.maximum(table_ref[(x * n_z + at) * capacity + k], 0)
            row = block // col_blocks
            col = block - row * col_blocks
            shift = lax.rem(x - row + n_x, n_x)
            value = pieces[0][col]
            for d in range(1, n_x):
                value = jnp.where(shift == d, pieces[d][col], value)
            out_ref[z, k] = value


def left_kernel(place_ref, grad_ref, left_ref, out_ref, grad, left, out, in_sem, out_sem):
    n_rep, capacity, band, width = out.shape
    shards, _, rows = grad.shape[:3]
    size = shards * rows
    piece = rows // n_rep
    half = n_rep // 2
    gets = []
    for k in range(capacity):
        if k == 0:
            for s in range(shards):
                at = along_z_place(s, shards, place_ref[1])
                gets.append(pltpu.make_async_copy(grad_ref.at[at], grad.at[s], in_sem.at[0, s]))
        for h in range(2):
            part = pl.ds(h * half, half)
            gets.append(
                pltpu.make_async_copy(left_ref.at[part, k], left.at[k, part], in_sem.at[1 + k, h])
            )
    for copy in gets:
        copy.start()
    for copy in gets[:shards]:
        copy.wait()
    for k in range(capacity):
        whole = grad[:, k].reshape(size, width)
        for h in range(2):
            gets[shards + 2 * k + h].wait()
            part = slice(h * half, (h + 1) * half)
            product = jnp.dot(
                left[k, part].reshape(half * band, size), whole, preferred_element_type=F32
            ).astype(BF16)
            product = product.reshape(half * band // rows, n_rep, piece, width)
            for r in range(n_rep):
                rows_r = slice(h * band // 2, (h + 1) * band // 2)
                out[REP_ORDER.index(r), k, rows_r] = product[:, r].reshape(band // 2, width)
        pltpu.make_async_copy(out.at[:, k], out_ref.at[:, k], out_sem.at[k]).start()
    for k in range(capacity):
        pltpu.make_async_copy(out.at[:, k], out_ref.at[:, k], out_sem.at[k]).wait()


def split3(value):
    high = value.astype(BF16).astype(F32)
    rest = value - high
    mid = rest.astype(BF16).astype(F32)
    return high, mid, rest - mid


def step_kernel(
    place_ref, table_ref, product_ref, right_ref, grad_ref, moment_ref, out_ref,
    product, right, grad, moment, out, in_sem, out_sem,
):
    n_rep, capacity, band, width = product.shape
    size = n_rep * width
    shards, _, piece = out.shape[:3]
    gets = []
    for s in range(shards):
        at = along_z_place(s, shards, place_ref[1])
        gets.append(pltpu.make_async_copy(grad_ref.at[at], grad.at[s], in_sem.at[0, s]))
    for p, r in enumerate(REP_ORDER):
        gets.append(pltpu.make_async_copy(moment_ref.at[p], moment.at[r], in_sem.at[1, r]))
    first = len(gets)
    half = n_rep // 2
    for k in range(capacity):
        if k == 0:
            gets.append(pltpu.make_async_copy(product_ref, product, in_sem.at[2, n_rep - 1]))
        for h in range(2):
            part = pl.ds(h * half, half)
            gets.append(
                pltpu.make_async_copy(
                    right_ref.at[part, capacity + k], right.at[k, part], in_sem.at[2 + k, h]
                )
            )
    for copy in gets:
        copy.start()
    for copy in gets[:first]:
        copy.wait()
    norms = []
    for k in range(capacity):
        live = table_ref[place_ref[3] * capacity + k] >= 0
        grad_k = grad[:, k].reshape(size, width).astype(F32)
        grad_k = jnp.where(live, grad_k, 0.0)
        moment_k = moment[:, k].reshape(size, width).astype(F32)
        moment_k = BETA_ADAM * moment_k + (1.0 - BETA_ADAM) * grad_k * grad_k
        step = grad_k / (jnp.sqrt(moment_k) + ADAM_EPS)
        norms.append(jnp.sum(step * step))
    gets[first].wait()
    for k in range(capacity):
        rows = jnp.concatenate(
            [product[REP_ORDER.index(r), k] for r in range(n_rep)], axis=1
        )
        for h in range(2):
            gets[first + 1 + 2 * k + h].wait()
        precond = jnp.dot(rows, right[k].reshape(size, size), preferred_element_type=F32)
        parts = split3(norms[k]) + split3(jnp.sum(precond * precond))
        lane = lax.broadcasted_iota(jnp.int32, (piece, PAD), 1)
        extra = jnp.zeros((piece, PAD), F32)
        for n, part in enumerate(parts):
            extra = jnp.where(lane == n, part, extra)
        extra = extra.astype(BF16)
        precond = precond.astype(BF16).reshape(shards, piece, size)
        for s in range(shards):
            at = along_z_place(s, shards, place_ref[1])
            out[at, k, :, :size] = precond[s]
            out[at, k, :, size:] = extra
        pltpu.make_async_copy(out.at[:, k], out_ref.at[:, k], out_sem.at[k]).start()
    for k in range(capacity):
        pltpu.make_async_copy(out.at[:, k], out_ref.at[:, k], out_sem.at[k]).wait()


def deal_kernel(place_ref, owner_ref, in_ref, after_ref, *out_refs):
    n_z, capacity = in_ref.shape[:2]
    n_x, col_blocks = len(out_refs), out_refs[0].shape[0]
    for d in range(n_x):
        row = lax.rem(place_ref[2] + d, n_x)
        for j in range(col_blocks):
            slot = owner_ref[row * col_blocks + j]
            owner = slot // capacity
            at = along_z_place(lax.rem(owner, n_z), n_z, place_ref[1])
            out_refs[d][j] = in_ref[at, lax.rem(slot, capacity)]


def collect_kernel(place_ref, owner_ref, *refs):
    pieces, out_ref = refs[:-1], refs[-1]
    n_x, col_blocks, _, width = len(pieces), *pieces[0].shape
    x = place_ref[2]
    for j in range(col_blocks):
        line = owner_ref[x * col_blocks + j] // place_ref[4]
        shift = lax.rem(x - line + n_x, n_x)
        value = pieces[0][j]
        for d in range(1, n_x):
            value = jnp.where(shift == d, pieces[d][j], value)
        out_ref[:, j * width : (j + 1) * width] = value


def stat_kernel(
    place_ref, table_ref, grad_ref, left_ref, right_ref, moment_ref,
    new_left_ref, new_right_ref, new_moment_ref, mark_ref, grad, sem,
):
    k = pl.program_id(0)
    n_rep, shards, _, rows, width = grad_ref.shape
    size = shards * rows
    rep = place_ref[0] * 2 + place_ref[1]
    copies = [
        pltpu.make_async_copy(
            grad_ref.at[r, s if r % 2 == 0 else shards - 1 - s, k],
            grad.at[s, :, pl.ds(r * width, width)],
            sem.at[r, s],
        )
        for r in range(n_rep)
        for s in range(shards)
    ]
    for copy in copies:
        copy.start()
    live = table_ref[place_ref[3] * pl.num_programs(0) + k] >= 0
    mark_ref[...] = jnp.zeros_like(mark_ref)
    for copy in copies:
        copy.wait()

    @pl.when(live)
    def _():
        whole = grad[...].reshape(size, size)
        band = grad[rep]
        gram = lax.dot_general(band, whole, (((1,), (1,)), ((), ())), preferred_element_type=F32)
        new_left_ref[0] = BETA_STAT * left_ref[0] + (1.0 - BETA_STAT) * gram
        cols = grad[:, :, column(rep, width)].reshape(size, width)
        gram = lax.dot_general(cols, whole, (((0,), (0,)), ((), ())), preferred_element_type=F32)
        new_right_ref[0] = BETA_STAT * right_ref[0] + (1.0 - BETA_STAT) * gram
        band = band.astype(F32)
        new_moment_ref[0] = BETA_ADAM * moment_ref[0] + (1.0 - BETA_ADAM) * band * band

    @pl.when(jnp.logical_not(live))
    def _():
        new_left_ref[0] = BETA_STAT * left_ref[0]
        new_right_ref[0] = BETA_STAT * right_ref[0]
        new_moment_ref[0] = BETA_ADAM * moment_ref[0]


def finish_kernel(order_ref, weights_ref, *refs):
    parts, out_ref, out, sem = refs[:-3], refs[-3], refs[-2], refs[-1]
    piece = parts[0].shape[0]
    col_blocks, width = sem.shape[0], parts[0].shape[1] // sem.shape[0]
    size = width - PAD
    lane = lax.broadcasted_iota(jnp.int32, (1, PAD), 1)
    copies = []
    for j in range(col_blocks):
        start = j * width
        extra = jnp.zeros((1, PAD), F32)
        for part in parts:
            extra += part[:1, start + size : start + width].astype(F32)
        adam = jnp.sum(jnp.where(lane < 3, extra, 0.0), axis=1, keepdims=True)
        norm = jnp.sum(jnp.where((lane >= 3) & (lane < 6), extra, 0.0), axis=1, keepdims=True)
        scale = -LEARN_RATE * jnp.sqrt(adam / (norm + NORM_EPS))
        cols = slice(j * size, (j + 1) * size)
        for n, part in enumerate(parts):
            rows = column(order_ref[n], piece)
            out[rows, cols] = (
                weights_ref[rows, cols].astype(F32)
                + scale * part[:, start : start + size].astype(F32)
            ).astype(BF16)
        copies.append(pltpu.make_async_copy(out.at[:, cols], out_ref.at[:, cols], sem.at[j]))
        copies[-1].start()
    for copy in copies:
        copy.wait()


def local(
    grad_parts, weights, left_stat, right_stat, left_root, right_root, adam_moment, owner_slot
):
    rep = lax.axis_index("rep")
    own = lax.axis_index("fsdp")
    n_rep, n_fsdp = lax.axis_size("rep"), lax.axis_size("fsdp")
    n_y, n_x = n_rep // 2, N_X
    n_z = n_fsdp // n_x
    capacity, band, size = left_stat.shape
    rows, full = grad_parts.shape[1:]
    col_blocks = full // size
    width = size // n_rep
    piece = rows // n_rep
    y, core, x = rep // 2, rep % 2, own // n_z
    place = jnp.stack([y, core, x, own, jnp.int32(n_z * capacity)]).astype(jnp.int32)
    slots = jnp.arange(n_fsdp * capacity, dtype=jnp.int32)
    blocks = jnp.arange(owner_slot.shape[0], dtype=jnp.int32)
    table = jnp.max(jnp.where(slots[:, None] == owner_slot[None, :], blocks[None, :], -1), axis=1)
    members = {0: range(n_z), 1: range(n_z - 1, -1, -1)}
    z_lines = [
        [(r * n_x + a) * n_z + b for b in members[r % 2]] for r in range(n_rep) for a in range(n_x)
    ]
    rep_lines = [[r * n_fsdp + a for r in REP_ORDER] for a in range(n_fsdp)]
    axes = ("rep", "fsdp")

    def along_y(value, shift):
        return lax.ppermute(value, "rep", [(i, (i + 2 * shift) % n_rep) for i in range(n_rep)])

    def across(value):
        return lax.ppermute(value, "rep", [(i, i ^ 1) for i in range(n_rep)])

    def along_x(value, shift):
        return lax.ppermute(
            value, "fsdp", [(i, (i + n_z * shift) % n_fsdp) for i in range(n_fsdp)]
        )

    def along_z(value):
        return lax.all_to_all(value, axes, 0, 0, tiled=True, axis_index_groups=z_lines)

    def over_rep(value):
        return lax.all_to_all(value, axes, 0, 0, tiled=True, axis_index_groups=rep_lines)

    roots = lax.all_gather(jnp.concatenate([left_root, right_root]), "rep", axis=0)

    shard = grad_parts[0]
    mine, other = pl.pallas_call(
        split_kernel,
        out_shape=[struct((n_y, col_blocks, rows, width))] * 2,
        in_specs=[SMEM, HBM],
        out_specs=[VMEM] * 2,
        scratch_shapes=[pltpu.SemaphoreType.DMA((2, n_y, col_blocks))],
        compiler_params=SMALL,
        name="split",
    )(place, shard)
    pairs = pl.pallas_call(
        pair_kernel,
        out_shape=[struct((col_blocks, rows, width))] * n_y,
        in_specs=[VMEM, VMEM],
        out_specs=[VMEM] * n_y,
        compiler_params=SMALL,
        name="pair",
    )(mine, across(other))
    terms = [pairs[0]] + [along_y(pairs[d], d) for d in range(1, n_y)]
    moment_cols = pl.pallas_call(
        turn_kernel,
        out_shape=struct((n_rep, capacity, band, width)),
        in_specs=[VMEM, ANY],
        out_specs=VMEM,
        compiler_params=SMALL,
        name="turn",
    )(adam_moment, pairs[0])
    summed = pl.pallas_call(
        sum_kernel,
        out_shape=struct((col_blocks, rows, width)),
        in_specs=[VMEM] * n_y + [ANY],
        out_specs=VMEM,
        compiler_params=SMALL,
        name="sum",
    )(*terms, moment_cols)
    moment_cols = over_rep(moment_cols)

    lines = [summed] + [along_x(summed, d) for d in range(1, n_x)]
    routed = along_z(
        pl.pallas_call(
            select_kernel,
            out_shape=struct((n_z, capacity, rows, width)),
            in_specs=[SMEM, SMEM] + [VMEM] * n_x + [ANY],
            out_specs=VMEM,
            compiler_params=SMALL,
            name="select",
        )(place, table, *lines, moment_cols)
    )

    product = pl.pallas_call(
        left_kernel,
        out_shape=struct((n_rep, capacity, band, width)),
        in_specs=[SMEM, ANY, HBM],
        out_specs=HBM,
        scratch_shapes=[
            pltpu.VMEM((n_z, capacity, rows, width), BF16),
            pltpu.VMEM((capacity, n_rep, band, size), BF16),
            pltpu.VMEM((n_rep, capacity, band, width), BF16),
            pltpu.SemaphoreType.DMA((1 + capacity, n_z)),
            pltpu.SemaphoreType.DMA((capacity,)),
        ],
        compiler_params=LARGE,
        name="left",
    )(place, routed, roots)
    product = over_rep(product)
    steps = pl.pallas_call(
        step_kernel,
        out_shape=struct((n_z, capacity, piece, size + PAD)),
        in_specs=[SMEM, SMEM, ANY, HBM, ANY, ANY],
        out_specs=HBM,
        scratch_shapes=[
            pltpu.VMEM((n_rep, capacity, band, width), BF16),
            pltpu.VMEM((capacity, n_rep, band, size), BF16),
            pltpu.VMEM((n_z, capacity, rows, width), BF16),
            pltpu.VMEM((n_rep, capacity, band, width), BF16),
            pltpu.VMEM((n_z, capacity, piece, size + PAD), BF16),
            pltpu.SemaphoreType.DMA((2 + capacity, n_rep)),
            pltpu.SemaphoreType.DMA((capacity,)),
        ],
        compiler_params=LARGE,
        name="step",
    )(place, table, product, roots, routed, moment_cols)

    gradient = lax.all_gather(routed, "rep", axis=0)
    stat = pl.BlockSpec((1, band, size), lambda k: (k, 0, 0))
    new_left, new_right, new_moment, mark = pl.pallas_call(
        stat_kernel,
        grid=(capacity,),
        out_shape=[struct(left_stat.shape, F32)] * 3 + [struct((8, PAD), F32)],
        in_specs=[SMEM, SMEM, HBM, stat, stat, stat],
        out_specs=[stat] * 3 + [pl.BlockSpec((8, PAD), lambda k: (0, 0))],
        scratch_shapes=[
            pltpu.VMEM((n_z, rows, size), BF16),
            pltpu.SemaphoreType.DMA((n_rep, n_z)),
        ],
        compiler_params=LARGE,
        cost_estimate=pl.CostEstimate(
            flops=8 * capacity * band * size * size,
            bytes_accessed=capacity * size * (24 * band + 2 * size),
            transcendentals=0,
        ),
        name="statistics",
    )(place, table, gradient, left_stat, right_stat, adam_moment)
    returned = along_z(steps)
    dealt = pl.pallas_call(
        deal_kernel,
        out_shape=[struct((col_blocks, piece, size + PAD))] * n_x,
        in_specs=[SMEM, SMEM, VMEM, ANY],
        out_specs=[VMEM] * n_x,
        compiler_params=SMALL,
        name="deal",
    )(place, owner_slot, returned, mark)
    dealt = [dealt[0]] + [along_x(dealt[d], d) for d in range(1, n_x)]
    update = pl.pallas_call(
        collect_kernel,
        out_shape=struct((piece, col_blocks * (size + PAD))),
        in_specs=[SMEM, SMEM] + [VMEM] * n_x,
        out_specs=VMEM,
        compiler_params=SMALL,
        name="collect",
    )(place, owner_slot, *dealt)
    held = [update] + [along_y(update, d) for d in range(1, n_y)]
    held += [across(value) for value in held]
    sources = [((y - d) % n_y) * 2 + core for d in range(n_y)]
    sources += [((y - d) % n_y) * 2 + 1 - core for d in range(n_y)]
    new_weights = pl.pallas_call(
        finish_kernel,
        out_shape=struct(weights.shape),
        in_specs=[SMEM] + [VMEM] * (1 + n_rep),
        out_specs=HBM,
        scratch_shapes=[pltpu.VMEM(weights.shape, BF16), pltpu.SemaphoreType.DMA((col_blocks,))],
        compiler_params=SMALL,
        name="finish",
    )(jnp.stack(sources).astype(jnp.int32), weights, *held)
    return (new_weights, new_left, new_right, new_moment)


def solution(mesh):
    return jax.shard_map(
        local,
        mesh=mesh,
        in_specs=(
            P("rep", "fsdp", None),
            P("fsdp", None),
            P("fsdp", "rep", None),
            P("fsdp", "rep", None),
            P("fsdp", "rep", None),
            P("fsdp", "rep", None),
            P("fsdp", "rep", None),
            P(),
        ),
        out_specs=(
            P("fsdp", None),
            P("fsdp", "rep", None),
            P("fsdp", "rep", None),
            P("fsdp", "rep", None),
        ),
        check_vma=False,
    )
```

```python
import jax
import jax.numpy as jnp
from jax import lax
from jax.experimental import pallas as pl
from jax.experimental.pallas import tpu as pltpu
from jax.sharding import PartitionSpec as P

BETA_STAT = 0.95
BETA_ADAM = 0.99
LEARN_RATE = 0.2
ADAM_EPS = 1e-08
NORM_EPS = 1e-06
PAD = 128
N_X = 4
ANY = pl.BlockSpec(memory_space=pl.ANY)
HBM = pl.BlockSpec(memory_space=pltpu.HBM)
SMEM = pl.BlockSpec(memory_space=pltpu.SMEM)
VMEM = pl.BlockSpec(memory_space=pltpu.VMEM)
SMALL = pltpu.CompilerParams(vmem_limit_bytes=16 * 1024 * 1024)
LARGE = pltpu.CompilerParams(vmem_limit_bytes=28 * 1024 * 1024)
WHOLE = pltpu.CompilerParams(vmem_limit_bytes=60 * 1024 * 1024)
BF16 = jnp.bfloat16
FREE = pl.CostEstimate(flops=1, bytes_accessed=1, transcendentals=0)
LONG = pl.CostEstimate(flops=9_200_000_000, bytes_accessed=1, transcendentals=0)
F32 = jnp.float32


def struct(shape, dtype=BF16):
    return jax.ShapeDtypeStruct(shape, dtype)


def along_z_place(z, n_z, core):
    return jnp.where(core == 0, z, n_z - 1 - z)


def chip_back(y, shift, n_y):
    return lax.rem(y - shift + n_y, n_y)


def column(index, width):
    return pl.ds(pl.multiple_of(index * width, width), width)


def split_kernel(place_ref, grad_ref, mine_ref, other_ref, sem):
    n_y, col_blocks, _, width = other_ref.shape
    y, core = place_ref[0], place_ref[1]
    copies = []
    for n, out_ref in enumerate((other_ref, mine_ref)):
        for d in range(n_y):
            for j in range(col_blocks):
                index = j * 2 * n_y + lax.rem(y + d, n_y) * 2 + (core if n else 1 - core)
                copies.append(
                    pltpu.make_async_copy(
                        grad_ref.at[:, column(index, width)], out_ref.at[d, j], sem.at[n, d, j]
                    )
                )
                copies[-1].start()
    for copy in copies:
        copy.wait()


def pair_kernel(mine_ref, got_ref, *out_refs):
    for d, out_ref in enumerate(out_refs):
        out_ref[...] = (mine_ref[d].astype(F32) + got_ref[d].astype(F32)).astype(BF16)


def sum_kernel(*refs):
    terms, out_ref = refs[:-1], refs[-1]
    total = terms[0][...].astype(F32)
    for term in terms[1:]:
        total += term[...].astype(F32)
    out_ref[...] = total.astype(BF16)


def gate_kernel(*refs):
    refs[-1][...] = jnp.zeros_like(refs[-1])


def right_split_kernel(place_ref, right_ref, after_ref, out_ref, sem):
    part = column(1 - place_ref[1], out_ref.shape[2])
    copy = pltpu.make_async_copy(right_ref.at[:, :, part], out_ref, sem)
    copy.start()
    copy.wait()


def join_kernel(place_ref, right_ref, got_ref, left_ref, after_ref, *refs):
    out_refs, sem = refs[:-1], refs[-1]
    n_y = len(out_refs)
    planes, band, half = out_refs[0].shape
    rows = band // 4
    part = column(place_ref[1], half)
    copies = []
    for d, out_ref in enumerate(out_refs):
        mine = column(lax.rem(place_ref[0] + d, n_y), rows)
        for k in range(2):
            copies.append((right_ref.at[k, :, part], out_ref.at[2 * k]))
            copies.append((got_ref.at[k], out_ref.at[2 * k + 1]))
            for h in range(2):
                copies.append(
                    (
                        left_ref.at[k, mine, pl.ds(h * half, half)],
                        out_ref.at[planes - 1, pl.ds((2 * k + h) * rows, rows)],
                    )
                )
    copies = [
        pltpu.make_async_copy(source, target, sem.at[n])
        for n, (source, target) in enumerate(copies)
    ]
    for copy in copies:
        copy.start()
    for copy in copies:
        copy.wait()


def moment_split_kernel(place_ref, moment_ref, after_ref, out_ref, sem):
    n_y, capacity, _, width = out_ref.shape
    copies = []
    for d in range(n_y):
        part = column(chip_back(place_ref[0], d, n_y) * 2 + 1 - place_ref[1], width)
        for k in range(capacity):
            copies.append(
                pltpu.make_async_copy(moment_ref.at[k, :, part], out_ref.at[d, k], sem.at[d, k])
            )
            copies[-1].start()
    for copy in copies:
        copy.wait()


def select_kernel(place_ref, table_ref, *refs):
    pieces, out_ref = refs[:-1], refs[-1]
    n_z, capacity = out_ref.shape[:2]
    n_x, col_blocks = len(pieces), pieces[0].shape[0]
    x = place_ref[2]
    for z in range(n_z):
        for k in range(capacity):
            at = along_z_place(z, n_z, place_ref[1])
            block = jnp.maximum(table_ref[(x * n_z + at) * capacity + k], 0)
            row = block // col_blocks
            col = block - row * col_blocks
            shift = lax.rem(x - row + n_x, n_x)
            value = pieces[0][col]
            for d in range(1, n_x):
                value = jnp.where(shift == d, pieces[d][col], value)
            out_ref[z, k] = value


def left_kernel(place_ref, *refs):
    grad_refs, (mine_ref, other_ref, out_ref, grad, left, out, grad_sem, in_sem, out_sem) = (
        refs[:-10],
        refs[-9:],
    )
    capacity, shards, rows, full = grad.shape
    n_y = len(grad_refs)
    width = full // n_y
    size = shards * rows
    gets = []
    half = left.shape[4] // 2
    group = left.shape[3]
    for rel, root_ref in enumerate((mine_ref, other_ref)):
        for k in range(capacity):
            for h in range(2):
                part = pl.ds((2 * k + h) * group, group)
                gets.append(
                    pltpu.make_async_copy(
                        root_ref.at[:, part],
                        left.at[rel, :, k, :, pl.ds(h * half, half)],
                        in_sem.at[rel, k, h],
                    )
                )
    for s in range(shards):
        at = along_z_place(s, shards, place_ref[1])
        for d in range(n_y):
            part = pl.ds(d * width, width)
            gets.append(
                pltpu.make_async_copy(
                    grad_refs[d].at[at], grad.at[:, s, :, part], grad_sem.at[s, d]
                )
            )
    for copy in gets:
        copy.start()
    for copy in gets:
        copy.wait()
    for k in range(capacity):
        product = jnp.dot(
            left[:, :, k].reshape(-1, size),
            grad[k].reshape(size, full),
            preferred_element_type=F32,
        )
        out[k] = product.astype(BF16)
        pltpu.make_async_copy(out.at[k], out_ref.at[k], out_sem.at[k]).start()
    for k in range(capacity):
        pltpu.make_async_copy(out.at[k], out_ref.at[k], out_sem.at[k]).wait()


def split3(value):
    high = value.astype(BF16).astype(F32)
    rest = value - high
    mid = rest.astype(BF16).astype(F32)
    return high, mid, rest - mid


def step_kernel(
    place_ref, table_ref, mine_ref, other_ref, moment_ref, got_ref, *refs
):
    n_y = (len(refs) - 9) // 2
    grad_refs, right_refs = refs[:n_y], refs[n_y : 2 * n_y]
    out_ref, product, right, grad, moment, out, near_sem, far_sem, out_sem = refs[2 * n_y :]
    _, capacity, group, half = product.shape
    shards, _, piece, padded = out.shape
    size = padded - PAD
    rows, width = grad.shape[3:]
    y, core = place_ref[0], place_ref[1]
    near = []
    far = []
    for rel in range(2):
        band = y * 2 + (core if rel == 0 else 1 - core)
        at = along_z_place(band, shards, core)
        for d in range(n_y):
            near.append(
                pltpu.make_async_copy(
                    grad_refs[d].at[at], grad.at[rel, d], near_sem.at[0, rel, d]
                )
            )
    for d in range(n_y):
        part = column(chip_back(y, d, n_y) * 2 + core, width)
        near.append(
            pltpu.make_async_copy(
                moment_ref.at[:, :, part], moment.at[0, d], near_sem.at[1, 0, d]
            )
        )
    near.append(pltpu.make_async_copy(got_ref, moment.at[1], near_sem.at[1, 1, 0]))
    far.append(pltpu.make_async_copy(mine_ref, product.at[0], near_sem.at[1, 1, 1]))
    for h in range(2):
        far.append(
            pltpu.make_async_copy(
                other_ref.at[:, pl.ds((1 - h) * (group // 2), group // 2)],
                product.at[1, :, pl.ds(h * (group // 2), group // 2)],
                near_sem.at[1, 1, 2 + h],
            )
        )
    for k in range(capacity):
        for d in range(n_y):
            far.append(
                pltpu.make_async_copy(
                    right_refs[d].at[pl.ds(2 * k, 2)], right.at[k, :, d], far_sem.at[k, d]
                )
            )
    for copy in near + far:
        copy.start()
    for copy in near:
        copy.wait()
    norms = []
    for k in range(capacity):
        live = table_ref[place_ref[3] * capacity + k] >= 0
        total = jnp.zeros((rows, width), F32)
        for rel in range(2):
            for d in range(n_y):
                grad_k = jnp.where(live, grad[rel, d, k].astype(F32), 0.0)
                moment_k = moment[rel, d, k]
                moment_k = BETA_ADAM * moment_k + (1.0 - BETA_ADAM) * grad_k * grad_k
                step = grad_k / (jnp.sqrt(moment_k) + ADAM_EPS)
                total += step * step
        norms.append(jnp.sum(total))
    for copy in far[:3]:
        copy.wait()
    lane = lax.broadcasted_iota(jnp.int32, (piece, PAD), 1)
    for k in range(capacity):
        for copy in far[3 + k * n_y : 3 + (k + 1) * n_y]:
            copy.wait()
        precond = jnp.dot(
            jnp.concatenate([product[0, k], product[1, k]], axis=1),
            right[k].reshape(size, half),
            preferred_element_type=F32,
        )
        parts = split3(norms[k]) + split3(jnp.sum(precond * precond))
        extra = jnp.zeros((piece, PAD), F32)
        for n, part in enumerate(parts):
            extra = jnp.where(lane == n, part, extra)
        extra = extra.astype(BF16)
        precond = precond.astype(BF16).reshape(2, n_y, 2, piece, half)
        for rel in range(2):
            for d in range(n_y):
                shard = chip_back(y, d, n_y) * 2 + (core if rel == 0 else 1 - core)
                at = along_z_place(shard, shards, core)
                out[at, k, :, :half] = precond[rel, d, 0]
                out[at, k, :, half:size] = precond[rel, d, 1]
                out[at, k, :, size:] = extra
        pltpu.make_async_copy(out.at[:, k], out_ref.at[:, k], out_sem.at[k]).start()
    for k in range(capacity):
        pltpu.make_async_copy(out.at[:, k], out_ref.at[:, k], out_sem.at[k]).wait()


def deal_kernel(place_ref, owner_ref, in_ref, *out_refs):
    n_z, capacity = in_ref.shape[:2]
    n_x, col_blocks = len(out_refs), out_refs[0].shape[0]
    for d in range(n_x):
        row = lax.rem(place_ref[2] + d, n_x)
        for j in range(col_blocks):
            slot = owner_ref[row * col_blocks + j]
            owner = slot // capacity
            at = along_z_place(lax.rem(owner, n_z), n_z, place_ref[1])
            out_refs[d][j] = in_ref[at, lax.rem(slot, capacity)]


def collect_kernel(place_ref, owner_ref, *refs):
    pieces, out_ref = refs[:-2], refs[-1]
    n_x, col_blocks, _, width = len(pieces), *pieces[0].shape
    x = place_ref[2]
    for j in range(col_blocks):
        line = owner_ref[x * col_blocks + j] // place_ref[4]
        shift = lax.rem(x - line + n_x, n_x)
        value = pieces[0][j]
        for d in range(1, n_x):
            value = jnp.where(shift == d, pieces[d][j], value)
        out_ref[:, j * width : (j + 1) * width] = value


def stat_kernel(place_ref, table_ref, *refs):
    grad_refs = refs[:-9]
    left_ref, right_ref, moment_ref = refs[-9:-6]
    new_left_ref, new_right_ref, new_moment_ref, mark_ref, grad, sem = refs[-6:]
    mark_ref[...] = jnp.zeros_like(mark_ref)
    k = pl.program_id(0)
    shards, rows, size = grad.shape
    n_y = len(grad_refs) // 2
    width = size // len(grad_refs)
    rep = place_ref[0] * 2 + place_ref[1]
    copies = []
    for n, grad_ref in enumerate(grad_refs):
        core = place_ref[1] if n < n_y else 1 - place_ref[1]
        part = column(chip_back(place_ref[0], n % n_y, n_y) * 2 + core, width)
        for s in range(shards):
            at = along_z_place(s, shards, core)
            copies.append(
                pltpu.make_async_copy(grad_ref.at[at, k], grad.at[s, :, part], sem.at[n, s])
            )
    for copy in copies:
        copy.start()
    live = table_ref[place_ref[3] * pl.num_programs(0) + k] >= 0
    for copy in copies:
        copy.wait()

    @pl.when(live)
    def _():
        whole = grad[...].reshape(size, size)
        band = grad[rep]
        gram = lax.dot_general(band, whole, (((1,), (1,)), ((), ())), preferred_element_type=F32)
        new_left_ref[0] = BETA_STAT * left_ref[0] + (1.0 - BETA_STAT) * gram
        cols = grad[:, :, column(rep, width)].reshape(size, width)
        gram = lax.dot_general(cols, whole, (((0,), (0,)), ((), ())), preferred_element_type=F32)
        new_right_ref[0] = BETA_STAT * right_ref[0] + (1.0 - BETA_STAT) * gram
        band = band.astype(F32)
        new_moment_ref[0] = BETA_ADAM * moment_ref[0] + (1.0 - BETA_ADAM) * band * band

    @pl.when(jnp.logical_not(live))
    def _():
        new_left_ref[0] = BETA_STAT * left_ref[0]
        new_right_ref[0] = BETA_STAT * right_ref[0]
        new_moment_ref[0] = BETA_ADAM * moment_ref[0]


def finish_kernel(order_ref, weights_ref, *refs):
    parts, out_ref, out, sem = refs[:-3], refs[-3], refs[-2], refs[-1]
    piece = parts[0].shape[0]
    col_blocks, width = sem.shape[0], parts[0].shape[1] // sem.shape[0]
    size = width - PAD
    lane = lax.broadcasted_iota(jnp.int32, (1, PAD), 1)
    copies = []
    for j in range(col_blocks):
        start = j * width
        extra = jnp.zeros((1, PAD), F32)
        for part in parts:
            extra += part[:1, start + size : start + width].astype(F32)
        adam = jnp.sum(jnp.where(lane < 3, extra, 0.0), axis=1, keepdims=True)
        norm = jnp.sum(jnp.where((lane >= 3) & (lane < 6), extra, 0.0), axis=1, keepdims=True)
        scale = -LEARN_RATE * jnp.sqrt(adam / (norm + NORM_EPS))
        cols = slice(j * size, (j + 1) * size)
        half = size // 2
        for n, part in enumerate(parts):
            side = pl.ds(pl.multiple_of(j * size + order_ref[2 * n + 1] * half, half), half)
            for h in range(2):
                rows = column(order_ref[2 * n] * 2 + h, piece)
                change = part[:, start + h * half : start + (h + 1) * half].astype(F32)
                out[rows, side] = (
                    weights_ref[rows, side].astype(F32) + scale * change
                ).astype(BF16)
        copies.append(pltpu.make_async_copy(out.at[:, cols], out_ref.at[:, cols], sem.at[j]))
        copies[-1].start()
    for copy in copies:
        copy.wait()


def local(
    grad_parts, weights, left_stat, right_stat, left_root, right_root, adam_moment, owner_slot
):
    rep = lax.axis_index("rep")
    own = lax.axis_index("fsdp")
    n_rep, n_fsdp = lax.axis_size("rep"), lax.axis_size("fsdp")
    n_y, n_x = n_rep // 2, N_X
    n_z = n_fsdp // n_x
    capacity, band, size = left_stat.shape
    rows, full = grad_parts.shape[1:]
    col_blocks = full // size
    width = size // n_rep
    piece = rows // n_rep
    y, core, x = rep // 2, rep % 2, own // n_z
    place = jnp.stack([y, core, x, own, jnp.int32(n_z * capacity)]).astype(jnp.int32)
    slots = jnp.arange(n_fsdp * capacity, dtype=jnp.int32)
    blocks = jnp.arange(owner_slot.shape[0], dtype=jnp.int32)
    table = jnp.max(jnp.where(slots[:, None] == owner_slot[None, :], blocks[None, :], -1), axis=1)
    members = {0: range(n_z), 1: range(n_z - 1, -1, -1)}
    z_lines = [
        [(r * n_x + a) * n_z + b for b in members[r % 2]] for r in range(n_rep) for a in range(n_x)
    ]
    axes = ("rep", "fsdp")

    def along_y(value, shift):
        return lax.ppermute(value, "rep", [(i, (i + 2 * shift) % n_rep) for i in range(n_rep)])

    def across(value):
        return lax.ppermute(value, "rep", [(i, i ^ 1) for i in range(n_rep)])

    def along_x(value, shift):
        return lax.ppermute(
            value, "fsdp", [(i, (i + n_z * shift) % n_fsdp) for i in range(n_fsdp)]
        )

    def along_z(value):
        return lax.all_to_all(value, axes, 0, 0, tiled=True, axis_index_groups=z_lines)

    shard = grad_parts[0]
    mine, other = pl.pallas_call(
        split_kernel,
        out_shape=[struct((n_y, col_blocks, rows, width))] * 2,
        in_specs=[SMEM, HBM],
        out_specs=[VMEM] * 2,
        scratch_shapes=[pltpu.SemaphoreType.DMA((2, n_y, col_blocks))],
        compiler_params=SMALL,
        cost_estimate=FREE,
        name="split",
    )(place, shard)
    pairs = pl.pallas_call(
        pair_kernel,
        out_shape=[struct((col_blocks, rows, width))] * n_y,
        in_specs=[VMEM, VMEM],
        out_specs=[VMEM] * n_y,
        compiler_params=SMALL,
        cost_estimate=FREE,
        name="pair",
    )(mine, across(other))
    terms = [pairs[0]] + [along_y(pairs[d], d) for d in range(1, n_y)]
    right_other = across(
        pl.pallas_call(
            right_split_kernel,
            out_shape=struct((capacity, band, size // 2)),
            in_specs=[SMEM, HBM, ANY],
            out_specs=VMEM,
            scratch_shapes=[pltpu.SemaphoreType.DMA],
            compiler_params=SMALL,
            cost_estimate=FREE,
            name="right_split",
        )(place, right_root, pairs[0])
    )
    moment_other = across(
        pl.pallas_call(
            moment_split_kernel,
            out_shape=struct((n_y, capacity, band, width), F32),
            in_specs=[SMEM, HBM, ANY],
            out_specs=VMEM,
            scratch_shapes=[pltpu.SemaphoreType.DMA((n_y, capacity))],
            compiler_params=SMALL,
            cost_estimate=FREE,
            name="moment_split",
        )(place, adam_moment, pairs[0])
    )
    summed = pl.pallas_call(
        sum_kernel,
        out_shape=struct((col_blocks, rows, width)),
        in_specs=[VMEM] * n_y,
        out_specs=VMEM,
        compiler_params=SMALL,
        cost_estimate=FREE,
        name="sum",
    )(*terms)
    roots = pl.pallas_call(
        join_kernel,
        out_shape=[struct((5, band, size // 2))] * n_y,
        in_specs=[SMEM] + [ANY] * 4,
        out_specs=[VMEM] * n_y,
        scratch_shapes=[pltpu.SemaphoreType.DMA((8 * n_y,))],
        compiler_params=SMALL,
        cost_estimate=FREE,
        name="join",
    )(place, right_root, right_other, left_root, pairs[0])
    roots = [roots[0]] + [along_y(roots[d], d) for d in range(1, n_y)]
    gate = pl.pallas_call(
        gate_kernel,
        out_shape=struct((8, PAD), F32),
        in_specs=[ANY] * (n_y - 1),
        out_specs=VMEM,
        compiler_params=SMALL,
        cost_estimate=LONG,
        name="gate",
    )(*roots[1:])

    lines = [summed] + [along_x(summed, d) for d in range(1, n_x)]
    routed = along_z(
        pl.pallas_call(
            select_kernel,
            out_shape=struct((n_z, capacity, rows, width)),
            in_specs=[SMEM, SMEM] + [VMEM] * n_x,
            out_specs=VMEM,
            compiler_params=SMALL,
            cost_estimate=FREE,
            name="select",
        )(place, table, *lines)
    )

    left_mine = jnp.stack([value[4] for value in roots])
    left_other = across(left_mine)
    routed, gate = lax.optimization_barrier((routed, gate))
    grads = [routed] + [along_y(routed, d) for d in range(1, n_y)]
    product = pl.pallas_call(
        left_kernel,
        out_shape=struct((capacity, 2 * band, size // 2)),
        in_specs=[SMEM] + [ANY] * (n_y + 3),
        out_specs=HBM,
        scratch_shapes=[
            pltpu.VMEM((capacity, n_z, rows, n_y * width), BF16),
            pltpu.VMEM((2, n_y, capacity, band // n_y, size), BF16),
            pltpu.VMEM((capacity, 2 * band, size // 2), BF16),
            pltpu.SemaphoreType.DMA((n_z, n_y)),
            pltpu.SemaphoreType.DMA((2, capacity, 2)),
            pltpu.SemaphoreType.DMA((capacity,)),
        ],
        compiler_params=LARGE,
        cost_estimate=FREE,
        name="left",
    )(place, *grads, gate, left_mine, left_other)
    steps = pl.pallas_call(
        step_kernel,
        out_shape=struct((n_z, capacity, piece, size + PAD)),
        in_specs=[SMEM, SMEM] + [ANY] * (4 + 2 * n_y),
        out_specs=HBM,
        scratch_shapes=[
            pltpu.VMEM((2, capacity, 2 * band, size // 2), BF16),
            pltpu.VMEM((capacity, 2, n_y, band, size // 2), BF16),
            pltpu.VMEM((2, n_y, capacity, rows, width), BF16),
            pltpu.VMEM((2, n_y, capacity, rows, width), F32),
            pltpu.VMEM((n_z, capacity, piece, size + PAD), BF16),
            pltpu.SemaphoreType.DMA((2, 2, n_y)),
            pltpu.SemaphoreType.DMA((capacity, n_y)),
            pltpu.SemaphoreType.DMA((capacity,)),
        ],
        compiler_params=LARGE,
        cost_estimate=FREE,
        name="step",
    )(place, table, product, across(product), adam_moment, moment_other, *grads, *roots)

    grads += [across(value) for value in grads]
    stat = pl.BlockSpec((1, band, size), lambda k: (k, 0, 0))
    new_left, new_right, new_moment, mark = pl.pallas_call(
        stat_kernel,
        grid=(capacity,),
        out_shape=[struct(left_stat.shape, F32)] * 3 + [struct((8, PAD), F32)],
        in_specs=[SMEM, SMEM] + [ANY] * n_rep + [stat] * 3,
        out_specs=[stat] * 3 + [pl.BlockSpec((8, PAD), lambda k: (0, 0))],
        scratch_shapes=[
            pltpu.VMEM((n_z, rows, size), BF16),
            pltpu.SemaphoreType.DMA((n_rep, n_z)),
        ],
        compiler_params=WHOLE,
        cost_estimate=FREE,
        name="statistics",
    )(place, table, *grads, left_stat, right_stat, adam_moment)
    returned = along_z(steps)
    dealt = pl.pallas_call(
        deal_kernel,
        out_shape=[struct((col_blocks, piece, size + PAD))] * n_x,
        in_specs=[SMEM, SMEM, VMEM],
        out_specs=[VMEM] * n_x,
        compiler_params=SMALL,
        cost_estimate=FREE,
        name="deal",
    )(place, owner_slot, returned)
    dealt = [dealt[0]] + [along_x(dealt[d], d) for d in range(1, n_x)]
    update = pl.pallas_call(
        collect_kernel,
        out_shape=struct((piece, col_blocks * (size + PAD))),
        in_specs=[SMEM, SMEM] + [VMEM] * n_x + [ANY],
        out_specs=VMEM,
        compiler_params=SMALL,
        cost_estimate=FREE,
        name="collect",
    )(place, owner_slot, *dealt, mark)
    held = [update] + [along_y(update, d) for d in range(1, n_y)]
    held += [across(value) for value in held]
    sources = []
    for side in (core, 1 - core):
        for d in range(n_y):
            sources += [(y - d) % n_y, side]
    new_weights = pl.pallas_call(
        finish_kernel,
        out_shape=struct(weights.shape),
        in_specs=[SMEM] + [VMEM] * (1 + n_rep),
        out_specs=HBM,
        scratch_shapes=[pltpu.VMEM(weights.shape, BF16), pltpu.SemaphoreType.DMA((col_blocks,))],
        compiler_params=SMALL,
        cost_estimate=FREE,
        name="finish",
    )(jnp.stack(sources).astype(jnp.int32), weights, *held)
    return (new_weights, new_left, new_right, new_moment)


def solution(mesh):
    return jax.shard_map(
        local,
        mesh=mesh,
        in_specs=(
            P("rep", "fsdp", None),
            P("fsdp", None),
            P("fsdp", "rep", None),
            P("fsdp", "rep", None),
            P("fsdp", "rep", None),
            P("fsdp", "rep", None),
            P("fsdp", "rep", None),
            P(),
        ),
        out_specs=(
            P("fsdp", None),
            P("fsdp", "rep", None),
            P("fsdp", "rep", None),
            P("fsdp", "rep", None),
        ),
        check_vma=False,
    )
```

```python
import jax
import jax.numpy as jnp
from jax import lax
from jax.experimental import pallas as pl
from jax.experimental.pallas import tpu as pltpu
from jax.sharding import PartitionSpec as P

BETA_STAT = 0.95
BETA_ADAM = 0.99
LEARN_RATE = 0.2
ADAM_EPS = 1e-08
NORM_EPS = 1e-06
PAD = 128
N_X = 4
ANY = pl.BlockSpec(memory_space=pl.ANY)
HBM = pl.BlockSpec(memory_space=pltpu.HBM)
SMEM = pl.BlockSpec(memory_space=pltpu.SMEM)
VMEM = pl.BlockSpec(memory_space=pltpu.VMEM)
SMALL = pltpu.CompilerParams(vmem_limit_bytes=16 * 1024 * 1024)
LARGE = pltpu.CompilerParams(vmem_limit_bytes=28 * 1024 * 1024)
WHOLE = pltpu.CompilerParams(vmem_limit_bytes=60 * 1024 * 1024)
BF16 = jnp.bfloat16
FREE = pl.CostEstimate(flops=1, bytes_accessed=1, transcendentals=0)
LONG = pl.CostEstimate(flops=9_200_000_000, bytes_accessed=1, transcendentals=0)
F32 = jnp.float32


def struct(shape, dtype=BF16):
    return jax.ShapeDtypeStruct(shape, dtype)


def along_z_place(z, n_z, core):
    return jnp.where(core == 0, z, n_z - 1 - z)


def chip_back(y, shift, n_y):
    return lax.rem(y - shift + n_y, n_y)


def column(index, width):
    return pl.ds(pl.multiple_of(index * width, width), width)


def split_kernel(place_ref, grad_ref, out_ref):
    n_y, col_blocks, _, width = out_ref.shape
    for d in range(n_y):
        chip = lax.rem(place_ref[0] + d, n_y)
        for j in range(col_blocks):
            index = (j * n_y + chip) * 2 + 1 - place_ref[1]
            out_ref[d, j] = grad_ref[:, column(index, width)]


def pair_kernel(place_ref, grad_ref, got_ref, *out_refs):
    n_y = len(out_refs)
    col_blocks, _, width = out_refs[0].shape
    for d, out_ref in enumerate(out_refs):
        chip = lax.rem(place_ref[0] + d, n_y)
        for j in range(col_blocks):
            index = (j * n_y + chip) * 2 + place_ref[1]
            mine = grad_ref[:, column(index, width)].astype(F32)
            out_ref[j] = (mine + got_ref[d, j].astype(F32)).astype(BF16)


def sum_kernel(*refs):
    terms, out_ref = refs[:-1], refs[-1]
    total = terms[0][...].astype(F32)
    for term in terms[1:]:
        total += term[...].astype(F32)
    out_ref[...] = total.astype(BF16)


def gate_kernel(*refs):
    refs[-1][...] = jnp.zeros_like(refs[-1])


def right_split_kernel(place_ref, right_ref, after_ref, out_ref, sem):
    part = column(1 - place_ref[1], out_ref.shape[2])
    copy = pltpu.make_async_copy(right_ref.at[:, :, part], out_ref, sem)
    copy.start()
    copy.wait()


def join_kernel(place_ref, right_ref, got_ref, left_ref, after_ref, *refs):
    out_refs, sem = refs[:-1], refs[-1]
    n_y = len(out_refs)
    planes, band, half = out_refs[0].shape
    rows = band // 4
    part = column(place_ref[1], half)
    copies = []
    for d, out_ref in enumerate(out_refs):
        mine = column(lax.rem(place_ref[0] + d, n_y), rows)
        for k in range(2):
            copies.append((right_ref.at[k, :, part], out_ref.at[2 * k]))
            copies.append((got_ref.at[k], out_ref.at[2 * k + 1]))
            for h in range(2):
                copies.append(
                    (
                        left_ref.at[k, mine, pl.ds(h * half, half)],
                        out_ref.at[planes - 1, pl.ds((2 * k + h) * rows, rows)],
                    )
                )
    copies = [
        pltpu.make_async_copy(source, target, sem.at[n])
        for n, (source, target) in enumerate(copies)
    ]
    for copy in copies:
        copy.start()
    for copy in copies:
        copy.wait()


def moment_split_kernel(place_ref, moment_ref, after_ref, out_ref, sem):
    n_y, capacity, _, width = out_ref.shape
    copies = []
    for d in range(n_y):
        part = column(chip_back(place_ref[0], d, n_y) * 2 + 1 - place_ref[1], width)
        for k in range(capacity):
            copies.append(
                pltpu.make_async_copy(moment_ref.at[k, :, part], out_ref.at[d, k], sem.at[d, k])
            )
            copies[-1].start()
    for copy in copies:
        copy.wait()


def select_kernel(place_ref, table_ref, *refs):
    pieces, out_ref = refs[:-1], refs[-1]
    n_z, capacity = out_ref.shape[:2]
    n_x, col_blocks = len(pieces), pieces[0].shape[0]
    x = place_ref[2]
    for z in range(n_z):
        for k in range(capacity):
            at = along_z_place(z, n_z, place_ref[1])
            block = jnp.maximum(table_ref[(x * n_z + at) * capacity + k], 0)
            row = block // col_blocks
            col = block - row * col_blocks
            shift = lax.rem(x - row + n_x, n_x)
            value = pieces[0][col]
            for d in range(1, n_x):
                value = jnp.where(shift == d, pieces[d][col], value)
            out_ref[z, k] = value


def left_kernel(place_ref, *refs):
    grad_refs, (mine_ref, other_ref, out_ref, grad, left, out, grad_sem, in_sem, out_sem) = (
        refs[:-10],
        refs[-9:],
    )
    capacity, shards, rows, full = grad.shape
    n_y = len(grad_refs)
    width = full // n_y
    size = shards * rows
    gets = []
    half = left.shape[4] // 2
    group = left.shape[3]
    for rel, root_ref in enumerate((mine_ref, other_ref)):
        for k in range(capacity):
            for h in range(2):
                part = pl.ds((2 * k + h) * group, group)
                gets.append(
                    pltpu.make_async_copy(
                        root_ref.at[:, part],
                        left.at[rel, :, k, :, pl.ds(h * half, half)],
                        in_sem.at[rel, k, h],
                    )
                )
    for s in range(shards):
        at = along_z_place(s, shards, place_ref[1])
        for d in range(n_y):
            part = pl.ds(d * width, width)
            gets.append(
                pltpu.make_async_copy(
                    grad_refs[d].at[at], grad.at[:, s, :, part], grad_sem.at[s, d]
                )
            )
    for copy in gets:
        copy.start()
    for copy in gets:
        copy.wait()
    for k in range(capacity):
        product = jnp.dot(
            left[:, :, k].reshape(-1, size),
            grad[k].reshape(size, full),
            preferred_element_type=F32,
        )
        out[k] = product.astype(BF16)
        pltpu.make_async_copy(out.at[k], out_ref.at[k], out_sem.at[k]).start()
    for k in range(capacity):
        pltpu.make_async_copy(out.at[k], out_ref.at[k], out_sem.at[k]).wait()


def split3(value):
    high = value.astype(BF16).astype(F32)
    rest = value - high
    mid = rest.astype(BF16).astype(F32)
    return high, mid, rest - mid


def step_kernel(
    place_ref, table_ref, mine_ref, other_ref, moment_ref, got_ref, *refs
):
    n_y = (len(refs) - 9) // 2
    grad_refs, right_refs = refs[:n_y], refs[n_y : 2 * n_y]
    out_ref, product, right, grad, moment, out, near_sem, far_sem, out_sem = refs[2 * n_y :]
    _, capacity, group, half = product.shape
    shards, _, piece, padded = out.shape
    size = padded - PAD
    rows, width = grad.shape[3:]
    y, core = place_ref[0], place_ref[1]
    near = []
    far = []
    for rel in range(2):
        band = y * 2 + (core if rel == 0 else 1 - core)
        at = along_z_place(band, shards, core)
        for d in range(n_y):
            near.append(
                pltpu.make_async_copy(
                    grad_refs[d].at[at], grad.at[rel, d], near_sem.at[0, rel, d]
                )
            )
    for d in range(n_y):
        part = column(chip_back(y, d, n_y) * 2 + core, width)
        near.append(
            pltpu.make_async_copy(
                moment_ref.at[:, :, part], moment.at[0, d], near_sem.at[1, 0, d]
            )
        )
    near.append(pltpu.make_async_copy(got_ref, moment.at[1], near_sem.at[1, 1, 0]))
    far.append(pltpu.make_async_copy(mine_ref, product.at[0], near_sem.at[1, 1, 1]))
    for h in range(2):
        far.append(
            pltpu.make_async_copy(
                other_ref.at[:, pl.ds((1 - h) * (group // 2), group // 2)],
                product.at[1, :, pl.ds(h * (group // 2), group // 2)],
                near_sem.at[1, 1, 2 + h],
            )
        )
    for k in range(capacity):
        for d in range(n_y):
            far.append(
                pltpu.make_async_copy(
                    right_refs[d].at[pl.ds(2 * k, 2)], right.at[k, :, d], far_sem.at[k, d]
                )
            )
    for copy in near + far:
        copy.start()
    for copy in near:
        copy.wait()
    norms = []
    for k in range(capacity):
        live = table_ref[place_ref[3] * capacity + k] >= 0
        total = jnp.zeros((rows, width), F32)
        for rel in range(2):
            for d in range(n_y):
                grad_k = jnp.where(live, grad[rel, d, k].astype(F32), 0.0)
                moment_k = moment[rel, d, k]
                moment_k = BETA_ADAM * moment_k + (1.0 - BETA_ADAM) * grad_k * grad_k
                step = grad_k / (jnp.sqrt(moment_k) + ADAM_EPS)
                total += step * step
        norms.append(jnp.sum(total))
    for copy in far[:3]:
        copy.wait()
    lane = lax.broadcasted_iota(jnp.int32, (piece, PAD), 1)
    for k in range(capacity):
        for copy in far[3 + k * n_y : 3 + (k + 1) * n_y]:
            copy.wait()
        precond = jnp.dot(
            jnp.concatenate([product[0, k], product[1, k]], axis=1),
            right[k].reshape(size, half),
            preferred_element_type=F32,
        )
        parts = split3(norms[k]) + split3(jnp.sum(precond * precond))
        extra = jnp.zeros((piece, PAD), F32)
        for n, part in enumerate(parts):
            extra = jnp.where(lane == n, part, extra)
        extra = extra.astype(BF16)
        precond = precond.astype(BF16).reshape(2, n_y, 2, piece, half)
        for rel in range(2):
            for d in range(n_y):
                shard = chip_back(y, d, n_y) * 2 + (core if rel == 0 else 1 - core)
                at = along_z_place(shard, shards, core)
                out[at, k, :, :half] = precond[rel, d, 0]
                out[at, k, :, half:size] = precond[rel, d, 1]
                out[at, k, :, size:] = extra
        pltpu.make_async_copy(out.at[:, k], out_ref.at[:, k], out_sem.at[k]).start()
    for k in range(capacity):
        pltpu.make_async_copy(out.at[:, k], out_ref.at[:, k], out_sem.at[k]).wait()


def deal_kernel(place_ref, owner_ref, in_ref, *out_refs):
    n_z, capacity = in_ref.shape[:2]
    n_x, col_blocks = len(out_refs), out_refs[0].shape[0]
    for d in range(n_x):
        row = lax.rem(place_ref[2] + d, n_x)
        for j in range(col_blocks):
            slot = owner_ref[row * col_blocks + j]
            owner = slot // capacity
            at = along_z_place(lax.rem(owner, n_z), n_z, place_ref[1])
            out_refs[d][j] = in_ref[at, lax.rem(slot, capacity)]


def collect_kernel(place_ref, owner_ref, *refs):
    pieces, out_ref = refs[:-2], refs[-1]
    n_x, col_blocks, _, width = len(pieces), *pieces[0].shape
    x = place_ref[2]
    for j in range(col_blocks):
        line = owner_ref[x * col_blocks + j] // place_ref[4]
        shift = lax.rem(x - line + n_x, n_x)
        value = pieces[0][j]
        for d in range(1, n_x):
            value = jnp.where(shift == d, pieces[d][j], value)
        out_ref[:, j * width : (j + 1) * width] = value


def stat_kernel(place_ref, table_ref, *refs):
    grad_refs = refs[:-9]
    left_ref, right_ref, moment_ref = refs[-9:-6]
    new_left_ref, new_right_ref, new_moment_ref, mark_ref, grad, sem = refs[-6:]
    mark_ref[...] = jnp.zeros_like(mark_ref)
    k = pl.program_id(0)
    shards, rows, size = grad.shape
    n_y = len(grad_refs) // 2
    width = size // len(grad_refs)
    rep = place_ref[0] * 2 + place_ref[1]
    copies = []
    for n, grad_ref in enumerate(grad_refs):
        core = place_ref[1] if n < n_y else 1 - place_ref[1]
        part = column(chip_back(place_ref[0], n % n_y, n_y) * 2 + core, width)
        for s in range(shards):
            at = along_z_place(s, shards, core)
            copies.append(
                pltpu.make_async_copy(grad_ref.at[at, k], grad.at[s, :, part], sem.at[n, s])
            )
    for copy in copies:
        copy.start()
    live = table_ref[place_ref[3] * pl.num_programs(0) + k] >= 0
    for copy in copies:
        copy.wait()

    @pl.when(live)
    def _():
        whole = grad[...].reshape(size, size)
        band = grad[rep]
        gram = lax.dot_general(band, whole, (((1,), (1,)), ((), ())), preferred_element_type=F32)
        new_left_ref[0] = BETA_STAT * left_ref[0] + (1.0 - BETA_STAT) * gram
        cols = grad[:, :, column(rep, width)].reshape(size, width)
        gram = lax.dot_general(cols, whole, (((0,), (0,)), ((), ())), preferred_element_type=F32)
        new_right_ref[0] = BETA_STAT * right_ref[0] + (1.0 - BETA_STAT) * gram
        band = band.astype(F32)
        new_moment_ref[0] = BETA_ADAM * moment_ref[0] + (1.0 - BETA_ADAM) * band * band

    @pl.when(jnp.logical_not(live))
    def _():
        new_left_ref[0] = BETA_STAT * left_ref[0]
        new_right_ref[0] = BETA_STAT * right_ref[0]
        new_moment_ref[0] = BETA_ADAM * moment_ref[0]


def finish_kernel(order_ref, weights_ref, *refs):
    parts, out_ref, out, sem = refs[:-3], refs[-3], refs[-2], refs[-1]
    piece = parts[0].shape[0]
    col_blocks, width = sem.shape[0], parts[0].shape[1] // sem.shape[0]
    size = width - PAD
    lane = lax.broadcasted_iota(jnp.int32, (1, PAD), 1)
    copies = []
    for j in range(col_blocks):
        start = j * width
        extra = jnp.zeros((1, PAD), F32)
        for part in parts:
            extra += part[:1, start + size : start + width].astype(F32)
        adam = jnp.sum(jnp.where(lane < 3, extra, 0.0), axis=1, keepdims=True)
        norm = jnp.sum(jnp.where((lane >= 3) & (lane < 6), extra, 0.0), axis=1, keepdims=True)
        scale = -LEARN_RATE * jnp.sqrt(adam / (norm + NORM_EPS))
        cols = slice(j * size, (j + 1) * size)
        half = size // 2
        for n, part in enumerate(parts):
            side = pl.ds(pl.multiple_of(j * size + order_ref[2 * n + 1] * half, half), half)
            for h in range(2):
                rows = column(order_ref[2 * n] * 2 + h, piece)
                change = part[:, start + h * half : start + (h + 1) * half].astype(F32)
                out[rows, side] = (
                    weights_ref[rows, side].astype(F32) + scale * change
                ).astype(BF16)
        copies.append(pltpu.make_async_copy(out.at[:, cols], out_ref.at[:, cols], sem.at[j]))
        copies[-1].start()
    for copy in copies:
        copy.wait()


def local(
    grad_parts, weights, left_stat, right_stat, left_root, right_root, adam_moment, owner_slot
):
    rep = lax.axis_index("rep")
    own = lax.axis_index("fsdp")
    n_rep, n_fsdp = lax.axis_size("rep"), lax.axis_size("fsdp")
    n_y, n_x = n_rep // 2, N_X
    n_z = n_fsdp // n_x
    capacity, band, size = left_stat.shape
    rows, full = grad_parts.shape[1:]
    col_blocks = full // size
    width = size // n_rep
    piece = rows // n_rep
    y, core, x = rep // 2, rep % 2, own // n_z
    place = jnp.stack([y, core, x, own, jnp.int32(n_z * capacity)]).astype(jnp.int32)
    slots = jnp.arange(n_fsdp * capacity, dtype=jnp.int32)
    blocks = jnp.arange(owner_slot.shape[0], dtype=jnp.int32)
    table = jnp.max(jnp.where(slots[:, None] == owner_slot[None, :], blocks[None, :], -1), axis=1)
    members = {0: range(n_z), 1: range(n_z - 1, -1, -1)}
    z_lines = [
        [(r * n_x + a) * n_z + b for b in members[r % 2]] for r in range(n_rep) for a in range(n_x)
    ]
    axes = ("rep", "fsdp")

    def along_y(value, shift):
        return lax.ppermute(value, "rep", [(i, (i + 2 * shift) % n_rep) for i in range(n_rep)])

    def across(value):
        return lax.ppermute(value, "rep", [(i, i ^ 1) for i in range(n_rep)])

    def along_x(value, shift):
        return lax.ppermute(
            value, "fsdp", [(i, (i + n_z * shift) % n_fsdp) for i in range(n_fsdp)]
        )

    def along_z(value):
        return lax.all_to_all(value, axes, 0, 0, tiled=True, axis_index_groups=z_lines)

    shard = grad_parts[0]
    other = pl.pallas_call(
        split_kernel,
        out_shape=struct((n_y, col_blocks, rows, width)),
        in_specs=[SMEM, VMEM],
        out_specs=VMEM,
        compiler_params=SMALL,
        cost_estimate=FREE,
        name="split",
    )(place, shard)
    pairs = pl.pallas_call(
        pair_kernel,
        out_shape=[struct((col_blocks, rows, width))] * n_y,
        in_specs=[SMEM, VMEM, VMEM],
        out_specs=[VMEM] * n_y,
        compiler_params=SMALL,
        cost_estimate=FREE,
        name="pair",
    )(place, shard, across(other))
    terms = [pairs[0]] + [along_y(pairs[d], d) for d in range(1, n_y)]
    right_other = across(
        pl.pallas_call(
            right_split_kernel,
            out_shape=struct((capacity, band, size // 2)),
            in_specs=[SMEM, HBM, ANY],
            out_specs=VMEM,
            scratch_shapes=[pltpu.SemaphoreType.DMA],
            compiler_params=SMALL,
            cost_estimate=FREE,
            name="right_split",
        )(place, right_root, owner_slot)
    )
    moment_other = across(
        pl.pallas_call(
            moment_split_kernel,
            out_shape=struct((n_y, capacity, band, width), F32),
            in_specs=[SMEM, HBM, ANY],
            out_specs=VMEM,
            scratch_shapes=[pltpu.SemaphoreType.DMA((n_y, capacity))],
            compiler_params=SMALL,
            cost_estimate=FREE,
            name="moment_split",
        )(place, adam_moment, pairs[0])
    )
    summed = pl.pallas_call(
        sum_kernel,
        out_shape=struct((col_blocks, rows, width)),
        in_specs=[VMEM] * n_y,
        out_specs=VMEM,
        compiler_params=SMALL,
        cost_estimate=FREE,
        name="sum",
    )(*terms)
    roots = pl.pallas_call(
        join_kernel,
        out_shape=[struct((5, band, size // 2))] * n_y,
        in_specs=[SMEM] + [ANY] * 4,
        out_specs=[VMEM] * n_y,
        scratch_shapes=[pltpu.SemaphoreType.DMA((8 * n_y,))],
        compiler_params=SMALL,
        cost_estimate=FREE,
        name="join",
    )(place, right_root, right_other, left_root, pairs[0])
    roots = list(roots)
    roots[2], summed = lax.optimization_barrier((roots[2], summed))
    roots = [roots[0]] + [along_y(roots[d], d) for d in range(1, n_y)]
    gate = pl.pallas_call(
        gate_kernel,
        out_shape=struct((8, PAD), F32),
        in_specs=[ANY] * (n_y - 1),
        out_specs=VMEM,
        compiler_params=SMALL,
        cost_estimate=LONG,
        name="gate",
    )(*roots[1:])

    lines = [summed] + [along_x(summed, d) for d in range(1, n_x)]
    routed = along_z(
        pl.pallas_call(
            select_kernel,
            out_shape=struct((n_z, capacity, rows, width)),
            in_specs=[SMEM, SMEM] + [VMEM] * n_x,
            out_specs=VMEM,
            compiler_params=SMALL,
            cost_estimate=FREE,
            name="select",
        )(place, table, *lines)
    )

    left_mine = jnp.stack([value[4] for value in roots])
    left_other = across(left_mine)
    routed, gate = lax.optimization_barrier((routed, gate))
    grads = [routed] + [along_y(routed, d) for d in range(1, n_y)]
    product = pl.pallas_call(
        left_kernel,
        out_shape=struct((capacity, 2 * band, size // 2)),
        in_specs=[SMEM] + [ANY] * (n_y + 3),
        out_specs=HBM,
        scratch_shapes=[
            pltpu.VMEM((capacity, n_z, rows, n_y * width), BF16),
            pltpu.VMEM((2, n_y, capacity, band // n_y, size), BF16),
            pltpu.VMEM((capacity, 2 * band, size // 2), BF16),
            pltpu.SemaphoreType.DMA((n_z, n_y)),
            pltpu.SemaphoreType.DMA((2, capacity, 2)),
            pltpu.SemaphoreType.DMA((capacity,)),
        ],
        compiler_params=LARGE,
        cost_estimate=FREE,
        name="left",
    )(place, *grads, gate, left_mine, left_other)
    steps = pl.pallas_call(
        step_kernel,
        out_shape=struct((n_z, capacity, piece, size + PAD)),
        in_specs=[SMEM, SMEM] + [ANY] * (4 + 2 * n_y),
        out_specs=HBM,
        scratch_shapes=[
            pltpu.VMEM((2, capacity, 2 * band, size // 2), BF16),
            pltpu.VMEM((capacity, 2, n_y, band, size // 2), BF16),
            pltpu.VMEM((2, n_y, capacity, rows, width), BF16),
            pltpu.VMEM((2, n_y, capacity, rows, width), F32),
            pltpu.VMEM((n_z, capacity, piece, size + PAD), BF16),
            pltpu.SemaphoreType.DMA((2, 2, n_y)),
            pltpu.SemaphoreType.DMA((capacity, n_y)),
            pltpu.SemaphoreType.DMA((capacity,)),
        ],
        compiler_params=LARGE,
        cost_estimate=FREE,
        name="step",
    )(place, table, product, across(product), adam_moment, moment_other, *grads, *roots)

    grads += [across(value) for value in grads]
    stat = pl.BlockSpec((1, band, size), lambda k: (k, 0, 0))
    new_left, new_right, new_moment, mark = pl.pallas_call(
        stat_kernel,
        grid=(capacity,),
        out_shape=[struct(left_stat.shape, F32)] * 3 + [struct((8, PAD), F32)],
        in_specs=[SMEM, SMEM] + [ANY] * n_rep + [stat] * 3,
        out_specs=[stat] * 3 + [pl.BlockSpec((8, PAD), lambda k: (0, 0))],
        scratch_shapes=[
            pltpu.VMEM((n_z, rows, size), BF16),
            pltpu.SemaphoreType.DMA((n_rep, n_z)),
        ],
        compiler_params=WHOLE,
        cost_estimate=FREE,
        name="statistics",
    )(place, table, *grads, left_stat, right_stat, adam_moment)
    returned = along_z(steps)
    dealt = pl.pallas_call(
        deal_kernel,
        out_shape=[struct((col_blocks, piece, size + PAD))] * n_x,
        in_specs=[SMEM, SMEM, VMEM],
        out_specs=[VMEM] * n_x,
        compiler_params=SMALL,
        cost_estimate=FREE,
        name="deal",
    )(place, owner_slot, returned)
    dealt = [dealt[0]] + [along_x(dealt[d], d) for d in range(1, n_x)]
    update = pl.pallas_call(
        collect_kernel,
        out_shape=struct((piece, col_blocks * (size + PAD))),
        in_specs=[SMEM, SMEM] + [VMEM] * n_x + [ANY],
        out_specs=VMEM,
        compiler_params=SMALL,
        cost_estimate=FREE,
        name="collect",
    )(place, owner_slot, *dealt, mark)
    held = [update] + [along_y(update, d) for d in range(1, n_y)]
    held += [across(value) for value in held]
    sources = []
    for side in (core, 1 - core):
        for d in range(n_y):
            sources += [(y - d) % n_y, side]
    new_weights = pl.pallas_call(
        finish_kernel,
        out_shape=struct(weights.shape),
        in_specs=[SMEM] + [VMEM] * (1 + n_rep),
        out_specs=HBM,
        scratch_shapes=[pltpu.VMEM(weights.shape, BF16), pltpu.SemaphoreType.DMA((col_blocks,))],
        compiler_params=SMALL,
        cost_estimate=FREE,
        name="finish",
    )(jnp.stack(sources).astype(jnp.int32), weights, *held)
    return (new_weights, new_left, new_right, new_moment)


def solution(mesh):
    return jax.shard_map(
        local,
        mesh=mesh,
        in_specs=(
            P("rep", "fsdp", None),
            P("fsdp", None),
            P("fsdp", "rep", None),
            P("fsdp", "rep", None),
            P("fsdp", "rep", None),
            P("fsdp", "rep", None),
            P("fsdp", "rep", None),
            P(),
        ),
        out_specs=(
            P("fsdp", None),
            P("fsdp", "rep", None),
            P("fsdp", "rep", None),
            P("fsdp", "rep", None),
        ),
        check_vma=False,
    )
```

```python
import jax
import jax.numpy as jnp
from jax import lax
from jax.experimental import pallas as pl
from jax.experimental.pallas import tpu as pltpu
from jax.sharding import PartitionSpec as P

BETA_STAT = 0.95
BETA_ADAM = 0.99
LEARN_RATE = 0.2
ADAM_EPS = 1e-08
NORM_EPS = 1e-06
PAD = 128
N_X = 4
ANY = pl.BlockSpec(memory_space=pl.ANY)
HBM = pl.BlockSpec(memory_space=pltpu.HBM)
SMEM = pl.BlockSpec(memory_space=pltpu.SMEM)
VMEM = pl.BlockSpec(memory_space=pltpu.VMEM)
SMALL = pltpu.CompilerParams(vmem_limit_bytes=16 * 1024 * 1024)
LARGE = pltpu.CompilerParams(vmem_limit_bytes=28 * 1024 * 1024)
WHOLE = pltpu.CompilerParams(vmem_limit_bytes=60 * 1024 * 1024)
BF16 = jnp.bfloat16
FREE = pl.CostEstimate(flops=1, bytes_accessed=1, transcendentals=0)
LONG = pl.CostEstimate(flops=9_200_000_000, bytes_accessed=1, transcendentals=0)
F32 = jnp.float32


def struct(shape, dtype=BF16):
    return jax.ShapeDtypeStruct(shape, dtype)


def along_z_place(z, n_z, core):
    return jnp.where(core == 0, z, n_z - 1 - z)


def chip_back(y, shift, n_y):
    return lax.rem(y - shift + n_y, n_y)


def column(index, width):
    return pl.ds(pl.multiple_of(index * width, width), width)


def split_kernel(place_ref, grad_ref, out_ref):
    n_y, col_blocks, _, width = out_ref.shape
    for d in range(n_y):
        chip = lax.rem(place_ref[0] + d, n_y)
        for j in range(col_blocks):
            index = (j * n_y + chip) * 2 + 1 - place_ref[1]
            out_ref[d, j] = grad_ref[:, column(index, width)]


def pair_kernel(place_ref, grad_ref, got_ref, *out_refs):
    n_y = len(out_refs)
    col_blocks, _, width = out_refs[0].shape
    for d, out_ref in enumerate(out_refs):
        chip = lax.rem(place_ref[0] + d, n_y)
        for j in range(col_blocks):
            index = (j * n_y + chip) * 2 + place_ref[1]
            mine = grad_ref[:, column(index, width)].astype(F32)
            out_ref[j] = (mine + got_ref[d, j].astype(F32)).astype(BF16)


def sum_kernel(*refs):
    terms, out_ref = refs[:-1], refs[-1]
    total = terms[0][...].astype(F32)
    for term in terms[1:]:
        total += term[...].astype(F32)
    out_ref[...] = total.astype(BF16)


def gate_kernel(*refs):
    refs[-1][...] = jnp.zeros_like(refs[-1])


def right_split_kernel(place_ref, right_ref, after_ref, out_ref, sem):
    part = column(1 - place_ref[1], out_ref.shape[2])
    copy = pltpu.make_async_copy(right_ref.at[:, :, part], out_ref, sem)
    copy.start()
    copy.wait()


def join_kernel(place_ref, right_ref, got_ref, left_ref, after_ref, *refs):
    out_refs, sem = refs[:-1], refs[-1]
    n_y = len(out_refs)
    planes, band, half = out_refs[0].shape
    rows = band // 4
    part = column(place_ref[1], half)
    copies = []
    for d, out_ref in enumerate(out_refs):
        mine = column(lax.rem(place_ref[0] + d, n_y), rows)
        for k in range(2):
            copies.append((right_ref.at[k, :, part], out_ref.at[2 * k]))
            copies.append((got_ref.at[k], out_ref.at[2 * k + 1]))
            for h in range(2):
                copies.append(
                    (
                        left_ref.at[k, mine, pl.ds(h * half, half)],
                        out_ref.at[planes - 1, pl.ds((2 * k + h) * rows, rows)],
                    )
                )
    copies = [
        pltpu.make_async_copy(source, target, sem.at[n])
        for n, (source, target) in enumerate(copies)
    ]
    for copy in copies:
        copy.start()
    for copy in copies:
        copy.wait()


def moment_split_kernel(place_ref, moment_ref, after_ref, out_ref, sem):
    n_y, capacity, _, width = out_ref.shape
    copies = []
    for d in range(n_y):
        part = column(chip_back(place_ref[0], d, n_y) * 2 + 1 - place_ref[1], width)
        for k in range(capacity):
            copies.append(
                pltpu.make_async_copy(moment_ref.at[k, :, part], out_ref.at[d, k], sem.at[d, k])
            )
            copies[-1].start()
    for copy in copies:
        copy.wait()


def select_kernel(place_ref, table_ref, *refs):
    pieces, out_ref = refs[:-1], refs[-1]
    n_z, capacity = out_ref.shape[:2]
    n_x, col_blocks = len(pieces), pieces[0].shape[0]
    x = place_ref[2]
    for z in range(n_z):
        for k in range(capacity):
            at = along_z_place(z, n_z, place_ref[1])
            block = jnp.maximum(table_ref[(x * n_z + at) * capacity + k], 0)
            row = block // col_blocks
            col = block - row * col_blocks
            shift = lax.rem(x - row + n_x, n_x)
            value = pieces[0][col]
            for d in range(1, n_x):
                value = jnp.where(shift == d, pieces[d][col], value)
            out_ref[z, k] = value


def left_kernel(place_ref, *refs):
    grad_refs, (mine_ref, other_ref, out_ref, grad, left, out, grad_sem, in_sem, out_sem) = (
        refs[:-10],
        refs[-9:],
    )
    capacity, shards, rows, full = grad.shape
    n_y = len(grad_refs)
    width = full // n_y
    size = shards * rows
    gets = []
    half = left.shape[4] // 2
    group = left.shape[3]
    for rel, root_ref in enumerate((mine_ref, other_ref)):
        for k in range(capacity):
            for h in range(2):
                part = pl.ds((2 * k + h) * group, group)
                gets.append(
                    pltpu.make_async_copy(
                        root_ref.at[:, part],
                        left.at[rel, :, k, :, pl.ds(h * half, half)],
                        in_sem.at[rel, k, h],
                    )
                )
    for s in range(shards):
        at = along_z_place(s, shards, place_ref[1])
        for d in range(n_y):
            part = pl.ds(d * width, width)
            gets.append(
                pltpu.make_async_copy(
                    grad_refs[d].at[at], grad.at[:, s, :, part], grad_sem.at[s, d]
                )
            )
    for copy in gets:
        copy.start()
    for copy in gets:
        copy.wait()
    for k in range(capacity):
        product = jnp.dot(
            left[:, :, k].reshape(-1, size),
            grad[k].reshape(size, full),
            preferred_element_type=F32,
        )
        out[k] = product.astype(BF16)
        pltpu.make_async_copy(out.at[k], out_ref.at[k], out_sem.at[k]).start()
    for k in range(capacity):
        pltpu.make_async_copy(out.at[k], out_ref.at[k], out_sem.at[k]).wait()


def split3(value):
    high = value.astype(BF16).astype(F32)
    rest = value - high
    mid = rest.astype(BF16).astype(F32)
    return high, mid, rest - mid


def step_kernel(
    place_ref, table_ref, mine_ref, other_ref, moment_ref, got_ref, *refs
):
    n_y = (len(refs) - 9) // 2
    grad_refs, right_refs = refs[:n_y], refs[n_y : 2 * n_y]
    out_ref, product, right, grad, moment, out, near_sem, far_sem, out_sem = refs[2 * n_y :]
    _, capacity, group, half = product.shape
    shards, _, piece, padded = out.shape
    size = padded - PAD
    rows, width = grad.shape[3:]
    y, core = place_ref[0], place_ref[1]
    near = []
    far = []
    for rel in range(2):
        band = y * 2 + (core if rel == 0 else 1 - core)
        at = along_z_place(band, shards, core)
        for d in range(n_y):
            near.append(
                pltpu.make_async_copy(
                    grad_refs[d].at[at], grad.at[rel, d], near_sem.at[0, rel, d]
                )
            )
    for d in range(n_y):
        part = column(chip_back(y, d, n_y) * 2 + core, width)
        near.append(
            pltpu.make_async_copy(
                moment_ref.at[:, :, part], moment.at[0, d], near_sem.at[1, 0, d]
            )
        )
    near.append(pltpu.make_async_copy(got_ref, moment.at[1], near_sem.at[1, 1, 0]))
    far.append(pltpu.make_async_copy(mine_ref, product.at[0], near_sem.at[1, 1, 1]))
    for h in range(2):
        far.append(
            pltpu.make_async_copy(
                other_ref.at[:, pl.ds((1 - h) * (group // 2), group // 2)],
                product.at[1, :, pl.ds(h * (group // 2), group // 2)],
                near_sem.at[1, 1, 2 + h],
            )
        )
    for k in range(capacity):
        for d in range(n_y):
            far.append(
                pltpu.make_async_copy(
                    right_refs[d].at[pl.ds(2 * k, 2)], right.at[k, :, d], far_sem.at[k, d]
                )
            )
    for copy in near + far:
        copy.start()
    for copy in near:
        copy.wait()
    norms = []
    for k in range(capacity):
        live = table_ref[place_ref[3] * capacity + k] >= 0
        total = jnp.zeros((rows, width), F32)
        for rel in range(2):
            for d in range(n_y):
                grad_k = jnp.where(live, grad[rel, d, k].astype(F32), 0.0)
                moment_k = moment[rel, d, k]
                moment_k = BETA_ADAM * moment_k + (1.0 - BETA_ADAM) * grad_k * grad_k
                step = grad_k / (jnp.sqrt(moment_k) + ADAM_EPS)
                total += step * step
        norms.append(jnp.sum(total))
    for copy in far[:3]:
        copy.wait()
    lane = lax.broadcasted_iota(jnp.int32, (piece, PAD), 1)
    for k in range(capacity):
        for copy in far[3 + k * n_y : 3 + (k + 1) * n_y]:
            copy.wait()
        precond = jnp.dot(
            jnp.concatenate([product[0, k], product[1, k]], axis=1),
            right[k].reshape(size, half),
            preferred_element_type=F32,
        )
        parts = split3(norms[k]) + split3(jnp.sum(precond * precond))
        extra = jnp.zeros((piece, PAD), F32)
        for n, part in enumerate(parts):
            extra = jnp.where(lane == n, part, extra)
        extra = extra.astype(BF16)
        precond = precond.astype(BF16).reshape(2, n_y, 2, piece, half)
        for rel in range(2):
            for d in range(n_y):
                shard = chip_back(y, d, n_y) * 2 + (core if rel == 0 else 1 - core)
                at = along_z_place(shard, shards, core)
                out[at, k, :, :half] = precond[rel, d, 0]
                out[at, k, :, half:size] = precond[rel, d, 1]
                out[at, k, :, size:] = extra
        pltpu.make_async_copy(out.at[:, k], out_ref.at[:, k], out_sem.at[k]).start()
    for k in range(capacity):
        pltpu.make_async_copy(out.at[:, k], out_ref.at[:, k], out_sem.at[k]).wait()


def deal_kernel(place_ref, owner_ref, in_ref, after_ref, *out_refs):
    n_z, capacity = in_ref.shape[:2]
    n_x, col_blocks = len(out_refs), out_refs[0].shape[0]
    for d in range(n_x):
        row = lax.rem(place_ref[2] + d, n_x)
        for j in range(col_blocks):
            slot = owner_ref[row * col_blocks + j]
            owner = slot // capacity
            at = along_z_place(lax.rem(owner, n_z), n_z, place_ref[1])
            out_refs[d][j] = in_ref[at, lax.rem(slot, capacity)]


def collect_kernel(place_ref, owner_ref, *refs):
    pieces, out_ref = refs[:-1], refs[-1]
    n_x, col_blocks, _, width = len(pieces), *pieces[0].shape
    x = place_ref[2]
    for j in range(col_blocks):
        line = owner_ref[x * col_blocks + j] // place_ref[4]
        shift = lax.rem(x - line + n_x, n_x)
        value = pieces[0][j]
        for d in range(1, n_x):
            value = jnp.where(shift == d, pieces[d][j], value)
        out_ref[:, j * width : (j + 1) * width] = value


def stat_kernel(place_ref, table_ref, *refs):
    grad_refs = refs[:-9]
    left_ref, right_ref, moment_ref = refs[-9:-6]
    new_left_ref, new_right_ref, new_moment_ref, mark_ref, grad, sem = refs[-6:]
    mark_ref[...] = jnp.zeros_like(mark_ref)
    k = pl.program_id(0)
    shards, rows, size = grad.shape
    n_y = len(grad_refs) // 2
    width = size // len(grad_refs)
    rep = place_ref[0] * 2 + place_ref[1]
    copies = []
    for n, grad_ref in enumerate(grad_refs):
        core = place_ref[1] if n < n_y else 1 - place_ref[1]
        part = column(chip_back(place_ref[0], n % n_y, n_y) * 2 + core, width)
        for s in range(shards):
            at = along_z_place(s, shards, core)
            copies.append(
                pltpu.make_async_copy(grad_ref.at[at, k], grad.at[s, :, part], sem.at[n, s])
            )
    for copy in copies:
        copy.start()
    live = table_ref[place_ref[3] * pl.num_programs(0) + k] >= 0
    for copy in copies:
        copy.wait()

    @pl.when(live)
    def _():
        whole = grad[...].reshape(size, size)
        band = grad[rep]
        gram = lax.dot_general(band, whole, (((1,), (1,)), ((), ())), preferred_element_type=F32)
        new_left_ref[0] = BETA_STAT * left_ref[0] + (1.0 - BETA_STAT) * gram
        cols = grad[:, :, column(rep, width)].reshape(size, width)
        gram = lax.dot_general(cols, whole, (((0,), (0,)), ((), ())), preferred_element_type=F32)
        new_right_ref[0] = BETA_STAT * right_ref[0] + (1.0 - BETA_STAT) * gram
        band = band.astype(F32)
        new_moment_ref[0] = BETA_ADAM * moment_ref[0] + (1.0 - BETA_ADAM) * band * band

    @pl.when(jnp.logical_not(live))
    def _():
        new_left_ref[0] = BETA_STAT * left_ref[0]
        new_right_ref[0] = BETA_STAT * right_ref[0]
        new_moment_ref[0] = BETA_ADAM * moment_ref[0]


def finish_kernel(order_ref, weights_ref, *refs):
    parts, out_ref, out, sem = refs[:-3], refs[-3], refs[-2], refs[-1]
    piece = parts[0].shape[0]
    col_blocks, width = sem.shape[0], parts[0].shape[1] // sem.shape[0]
    size = width - PAD
    lane = lax.broadcasted_iota(jnp.int32, (1, PAD), 1)
    copies = []
    for j in range(col_blocks):
        start = j * width
        extra = jnp.zeros((1, PAD), F32)
        for part in parts:
            extra += part[:1, start + size : start + width].astype(F32)
        adam = jnp.sum(jnp.where(lane < 3, extra, 0.0), axis=1, keepdims=True)
        norm = jnp.sum(jnp.where((lane >= 3) & (lane < 6), extra, 0.0), axis=1, keepdims=True)
        scale = -LEARN_RATE * jnp.sqrt(adam / (norm + NORM_EPS))
        cols = slice(j * size, (j + 1) * size)
        half = size // 2
        for n, part in enumerate(parts):
            side = pl.ds(pl.multiple_of(j * size + order_ref[2 * n + 1] * half, half), half)
            for h in range(2):
                rows = column(order_ref[2 * n] * 2 + h, piece)
                change = part[:, start + h * half : start + (h + 1) * half].astype(F32)
                out[rows, side] = (
                    weights_ref[rows, side].astype(F32) + scale * change
                ).astype(BF16)
        copies.append(pltpu.make_async_copy(out.at[:, cols], out_ref.at[:, cols], sem.at[j]))
        copies[-1].start()
    for copy in copies:
        copy.wait()


def local(
    grad_parts, weights, left_stat, right_stat, left_root, right_root, adam_moment, owner_slot
):
    rep = lax.axis_index("rep")
    own = lax.axis_index("fsdp")
    n_rep, n_fsdp = lax.axis_size("rep"), lax.axis_size("fsdp")
    n_y, n_x = n_rep // 2, N_X
    n_z = n_fsdp // n_x
    capacity, band, size = left_stat.shape
    rows, full = grad_parts.shape[1:]
    col_blocks = full // size
    width = size // n_rep
    piece = rows // n_rep
    y, core, x = rep // 2, rep % 2, own // n_z
    place = jnp.stack([y, core, x, own, jnp.int32(n_z * capacity)]).astype(jnp.int32)
    slots = jnp.arange(n_fsdp * capacity, dtype=jnp.int32)
    blocks = jnp.arange(owner_slot.shape[0], dtype=jnp.int32)
    table = jnp.max(jnp.where(slots[:, None] == owner_slot[None, :], blocks[None, :], -1), axis=1)
    members = {0: range(n_z), 1: range(n_z - 1, -1, -1)}
    z_lines = [
        [(r * n_x + a) * n_z + b for b in members[r % 2]] for r in range(n_rep) for a in range(n_x)
    ]
    axes = ("rep", "fsdp")

    def along_y(value, shift):
        return lax.ppermute(value, "rep", [(i, (i + 2 * shift) % n_rep) for i in range(n_rep)])

    def across(value):
        return lax.ppermute(value, "rep", [(i, i ^ 1) for i in range(n_rep)])

    def along_x(value, shift):
        return lax.ppermute(
            value, "fsdp", [(i, (i + n_z * shift) % n_fsdp) for i in range(n_fsdp)]
        )

    def along_z(value):
        return lax.all_to_all(value, axes, 0, 0, tiled=True, axis_index_groups=z_lines)

    shard = grad_parts[0]
    other = pl.pallas_call(
        split_kernel,
        out_shape=struct((n_y, col_blocks, rows, width)),
        in_specs=[SMEM, VMEM],
        out_specs=VMEM,
        compiler_params=SMALL,
        cost_estimate=FREE,
        name="split",
    )(place, shard)
    pairs = pl.pallas_call(
        pair_kernel,
        out_shape=[struct((col_blocks, rows, width))] * n_y,
        in_specs=[SMEM, VMEM, VMEM],
        out_specs=[VMEM] * n_y,
        compiler_params=SMALL,
        cost_estimate=FREE,
        name="pair",
    )(place, shard, across(other))
    terms = [pairs[0]] + [along_y(pairs[d], d) for d in range(1, n_y)]
    right_other = across(
        pl.pallas_call(
            right_split_kernel,
            out_shape=struct((capacity, band, size // 2)),
            in_specs=[SMEM, HBM, ANY],
            out_specs=VMEM,
            scratch_shapes=[pltpu.SemaphoreType.DMA],
            compiler_params=SMALL,
            cost_estimate=FREE,
            name="right_split",
        )(place, right_root, owner_slot)
    )
    moment_other = across(
        pl.pallas_call(
            moment_split_kernel,
            out_shape=struct((n_y, capacity, band, width), F32),
            in_specs=[SMEM, HBM, ANY],
            out_specs=VMEM,
            scratch_shapes=[pltpu.SemaphoreType.DMA((n_y, capacity))],
            compiler_params=SMALL,
            cost_estimate=FREE,
            name="moment_split",
        )(place, adam_moment, pairs[0])
    )
    summed = pl.pallas_call(
        sum_kernel,
        out_shape=struct((col_blocks, rows, width)),
        in_specs=[VMEM] * n_y,
        out_specs=VMEM,
        compiler_params=SMALL,
        cost_estimate=FREE,
        name="sum",
    )(*terms)
    roots = pl.pallas_call(
        join_kernel,
        out_shape=[struct((5, band, size // 2))] * n_y,
        in_specs=[SMEM] + [ANY] * 4,
        out_specs=[VMEM] * n_y,
        scratch_shapes=[pltpu.SemaphoreType.DMA((8 * n_y,))],
        compiler_params=SMALL,
        cost_estimate=FREE,
        name="join",
    )(place, right_root, right_other, left_root, pairs[0])
    roots = list(roots)
    roots[2], summed = lax.optimization_barrier((roots[2], summed))
    roots = [roots[0]] + [along_y(roots[d], d) for d in range(1, n_y)]
    gate = pl.pallas_call(
        gate_kernel,
        out_shape=struct((8, PAD), F32),
        in_specs=[ANY] * (n_y - 1),
        out_specs=VMEM,
        compiler_params=SMALL,
        cost_estimate=LONG,
        name="gate",
    )(*roots[1:])

    lines = [summed] + [along_x(summed, d) for d in range(1, n_x)]
    routed = along_z(
        pl.pallas_call(
            select_kernel,
            out_shape=struct((n_z, capacity, rows, width)),
            in_specs=[SMEM, SMEM] + [VMEM] * n_x,
            out_specs=VMEM,
            compiler_params=SMALL,
            cost_estimate=FREE,
            name="select",
        )(place, table, *lines)
    )

    left_mine = jnp.stack([value[4] for value in roots])
    left_other = across(left_mine)
    routed, gate = lax.optimization_barrier((routed, gate))
    grads = [routed] + [along_y(routed, d) for d in range(1, n_y)]
    product = pl.pallas_call(
        left_kernel,
        out_shape=struct((capacity, 2 * band, size // 2)),
        in_specs=[SMEM] + [ANY] * (n_y + 3),
        out_specs=HBM,
        scratch_shapes=[
            pltpu.VMEM((capacity, n_z, rows, n_y * width), BF16),
            pltpu.VMEM((2, n_y, capacity, band // n_y, size), BF16),
            pltpu.VMEM((capacity, 2 * band, size // 2), BF16),
            pltpu.SemaphoreType.DMA((n_z, n_y)),
            pltpu.SemaphoreType.DMA((2, capacity, 2)),
            pltpu.SemaphoreType.DMA((capacity,)),
        ],
        compiler_params=LARGE,
        cost_estimate=FREE,
        name="left",
    )(place, *grads, gate, left_mine, left_other)
    steps = pl.pallas_call(
        step_kernel,
        out_shape=struct((n_z, capacity, piece, size + PAD)),
        in_specs=[SMEM, SMEM] + [ANY] * (4 + 2 * n_y),
        out_specs=HBM,
        scratch_shapes=[
            pltpu.VMEM((2, capacity, 2 * band, size // 2), BF16),
            pltpu.VMEM((capacity, 2, n_y, band, size // 2), BF16),
            pltpu.VMEM((2, n_y, capacity, rows, width), BF16),
            pltpu.VMEM((2, n_y, capacity, rows, width), F32),
            pltpu.VMEM((n_z, capacity, piece, size + PAD), BF16),
            pltpu.SemaphoreType.DMA((2, 2, n_y)),
            pltpu.SemaphoreType.DMA((capacity, n_y)),
            pltpu.SemaphoreType.DMA((capacity,)),
        ],
        compiler_params=LARGE,
        cost_estimate=FREE,
        name="step",
    )(place, table, product, across(product), adam_moment, moment_other, *grads, *roots)

    grads += [across(value) for value in grads]
    stat = pl.BlockSpec((1, band, size), lambda k: (k, 0, 0))
    new_left, new_right, new_moment, mark = pl.pallas_call(
        stat_kernel,
        grid=(capacity,),
        out_shape=[struct(left_stat.shape, F32)] * 3 + [struct((8, PAD), F32)],
        in_specs=[SMEM, SMEM] + [ANY] * n_rep + [stat] * 3,
        out_specs=[stat] * 3 + [pl.BlockSpec((8, PAD), lambda k: (0, 0))],
        scratch_shapes=[
            pltpu.VMEM((n_z, rows, size), BF16),
            pltpu.SemaphoreType.DMA((n_rep, n_z)),
        ],
        compiler_params=WHOLE,
        cost_estimate=FREE,
        name="statistics",
    )(place, table, *grads, left_stat, right_stat, adam_moment)
    returned = along_z(steps)
    dealt = pl.pallas_call(
        deal_kernel,
        out_shape=[struct((col_blocks, piece, size + PAD))] * n_x,
        in_specs=[SMEM, SMEM, VMEM, ANY],
        out_specs=[VMEM] * n_x,
        compiler_params=SMALL,
        cost_estimate=FREE,
        name="deal",
    )(place, owner_slot, returned, mark)
    dealt = [dealt[0]] + [along_x(dealt[d], d) for d in range(1, n_x)]
    update = pl.pallas_call(
        collect_kernel,
        out_shape=struct((piece, col_blocks * (size + PAD))),
        in_specs=[SMEM, SMEM] + [VMEM] * n_x,
        out_specs=VMEM,
        compiler_params=SMALL,
        cost_estimate=FREE,
        name="collect",
    )(place, owner_slot, *dealt)
    held = [update] + [along_y(update, d) for d in range(1, n_y)]
    held += [across(value) for value in held]
    sources = []
    for side in (core, 1 - core):
        for d in range(n_y):
            sources += [(y - d) % n_y, side]
    new_weights = pl.pallas_call(
        finish_kernel,
        out_shape=struct(weights.shape),
        in_specs=[SMEM] + [VMEM] * (1 + n_rep),
        out_specs=HBM,
        scratch_shapes=[pltpu.VMEM(weights.shape, BF16), pltpu.SemaphoreType.DMA((col_blocks,))],
        compiler_params=SMALL,
        cost_estimate=FREE,
        name="finish",
    )(jnp.stack(sources).astype(jnp.int32), weights, *held)
    return (new_weights, new_left, new_right, new_moment)


def solution(mesh):
    return jax.shard_map(
        local,
        mesh=mesh,
        in_specs=(
            P("rep", "fsdp", None),
            P("fsdp", None),
            P("fsdp", "rep", None),
            P("fsdp", "rep", None),
            P("fsdp", "rep", None),
            P("fsdp", "rep", None),
            P("fsdp", "rep", None),
            P(),
        ),
        out_specs=(
            P("fsdp", None),
            P("fsdp", "rep", None),
            P("fsdp", "rep", None),
            P("fsdp", "rep", None),
        ),
        check_vma=False,
    )
```
